512 devices in a mesh: strip: 32 (over z, core), pt: 16 (over x, y).
Axes of the slice: x: 4, y: 4, z: 16, core: 2. Of those that a mesh axis runs over, the one named last changes fastest.
Arguments:
- spectra: float32 [600, 128, 4096], P(None, 'strip', 'pt'), may hold values from 0.01 to 1
- courant: float32 [25], replicated, may hold values from 0.05 to 0.4
- wind_speed: float32 [128, 4096], P('strip', 'pt'), may hold values from 0.5 to 2
- wind_dir: float32 [128, 4096], P('strip', 'pt'), may hold values from -3.140625 to 3.140625
- sea_mask: int32 [128, 4096], P('strip', 'pt'), may hold values 0 or 1
- ice_mask: int32 [128, 4096], P('strip', 'pt'), may hold values 0 or 1
Outputs:
- new_spectra: float32 [600, 128, 4096], P(None, 'strip', 'pt')
The draws below stay inside these ranges and needn't reach their ends.
All inputs are finite; a program needn't handle non-finite values. No bound on the sum of `sea_mask` or of `ice_mask` on one device may be relied on, other than what follows from the above.
Results may differ from the reference program's by a relative error of at most 0.000088.
Values sent between devices are 32-bit elements; how exact they have to be, the bound alone decides.
No kernel may reach another device: no remote copies, remote signals or barrier semaphores. Data moves between devices by JAX's collectives and lax.ppermute only.
A program may use at most 64 MiB of HBM per device.

```python
import math
import jax
import jax.numpy as jnp
from jax import lax

NF = 25
ND = 24
SUB = 2
K = 600
NY = 128
NX = 4096


def place_ends(result, own_key, least, high):
    shape = result.shape
    index_at = [jax.random.randint(jax.random.fold_in(own_key, axis), (), 0, shape[axis]) for axis in range(len(shape))]
    result = result.at[tuple(index_at)].set(least)
    longest = shape.index(max(shape))
    index_at[longest] = (index_at[longest] + 1) % shape[longest]
    return result.at[tuple(index_at)].set(high)


def levels(key, shape, pieces, low, largest):
    def one(dim, blocks):
        draws = jax.random.uniform(jax.random.fold_in(jax.random.fold_in(key, 6), dim), (blocks,), jnp.float32, low / len(pieces), largest / len(pieces))
        return jnp.repeat(jnp.exp(draws), shape[dim] // blocks).reshape((-1,) + (1,) * (len(shape) - dim - 1))

    factor_of = one(*pieces[0])
    for cut in pieces[1:]:
        factor_of = factor_of * one(*cut)
    return factor_of


def setup_inputs(seed: int = 0) -> dict:
    key_list = jax.random.split(jax.random.key(seed), 7)
    return {
        "spectra": jnp.clip(jnp.exp(math.log(1.0) - 4.6051702 * jax.random.uniform(key_list[0], (K, NY, NX), jnp.float32) ** levels(key_list[0], (K, NY, NX), ((1, 32), (2, 16)), -0.2, 0.2)), 0.01, 1.0),
        "courant": jnp.clip(jnp.exp(jax.random.uniform(key_list[1], (NF,), jnp.float32, math.log(0.05), math.log(0.4))), 0.05, 0.4),
        "wind_speed": jnp.clip(jnp.exp(math.log(2.0) - 1.3862944 * jax.random.uniform(key_list[2], (NY, NX), jnp.float32) ** levels(key_list[2], (NY, NX), ((0, 32), (1, 16)), -0.2, 0.2)), 0.5, 2.0),
        "wind_dir": jnp.clip(jax.random.uniform(key_list[3], (NY, NX), jnp.float32, -3.140625, 3.140625), -3.140625, 3.140625),
        "sea_mask": place_ends((jax.random.randint(key_list[4], (NY, NX), 0, 4) < 3).astype(jnp.int32), jax.random.fold_in(key_list[4], 1), 0, 1),
        "ice_mask": place_ends((jax.random.randint(key_list[5], (NY, NX), 0, 8) < 1).astype(jnp.int32), jax.random.fold_in(key_list[5], 1), 0, 1),
    }


def tables(courant):
    ratio = 1.1 ** jnp.arange(NF, dtype=jnp.float32)
    theta = 2.0 * jnp.pi * jnp.arange(ND, dtype=jnp.float32) / ND
    speed_u = (courant[:, None] * jnp.cos(theta)[None, :]).reshape(-1)
    speed_v = (courant[:, None] * jnp.sin(theta)[None, :]).reshape(-1)
    return ratio, theta, speed_u, speed_v


def advance(core, west, east, south, north, speed_u, speed_v, sea):
    up_pos = jnp.maximum(speed_u, 0.0)[:, None, None]
    up_neg = jnp.minimum(speed_u, 0.0)[:, None, None]
    vp_pos = jnp.maximum(speed_v, 0.0)[:, None, None]
    vp_neg = jnp.minimum(speed_v, 0.0)[:, None, None]
    fresh = core - up_pos * (core - west) - up_neg * (east - core) - vp_pos * (core - south) - vp_neg * (north - core)
    return fresh * sea


def source(energy, wind_speed, wind_dir, ice_mask, ratio, theta):
    rows = energy.shape[1]
    cols = energy.shape[2]
    field = energy.reshape(NF, ND, rows, cols)
    weight = ratio / (ND * jnp.sum(ratio))
    first = jnp.einsum("fdyx,f->yx", field, weight, precision=lax.Precision.HIGHEST)
    second = jnp.einsum("fdyx,f->yx", field, weight * ratio, precision=lax.Precision.HIGHEST)
    mean_ratio = second / jnp.maximum(first, 0.05)
    icef = ice_mask.astype(jnp.float32)
    align = jnp.maximum(jnp.cos(theta[:, None, None] - wind_dir[None]), 0.0)
    gain = 0.05 * wind_speed[None, None] * ratio[:, None, None, None] * align[None]
    loss = 0.02 * ratio[:, None, None, None] * mean_ratio[None, None]
    net = (1.0 - icef)[None, None] * gain - loss - 0.7 * icef[None, None]
    return (field * jnp.exp(net)).reshape(NF * ND, rows, cols)


def propagate_band(block, speed_u, speed_v, sea):
    for step in range(SUB):
        zero_row = jnp.zeros((block.shape[0], 1, block.shape[2]), jnp.float32)
        south = jnp.concatenate([zero_row, block[:, :-1]], axis=1)
        north = jnp.concatenate([block[:, 1:], zero_row], axis=1)
        west = jnp.roll(block, 1, axis=2)
        east = jnp.roll(block, -1, axis=2)
        block = advance(block, west, east, south, north, speed_u, speed_v, sea[None])
    return block


def reference(spectra, courant, wind_speed, wind_dir, sea_mask, ice_mask):
    ratio, theta, speed_u, speed_v = tables(courant)
    sea = sea_mask.astype(jnp.float32)
    grouped = spectra.reshape(NF, ND, spectra.shape[1], spectra.shape[2])
    moved = lax.map(lambda item: propagate_band(item[0], item[1], item[2], sea),
                    (grouped, speed_u.reshape(NF, ND), speed_v.reshape(NF, ND)))
    energy = moved.reshape(NF * ND, spectra.shape[1], spectra.shape[2])
    by_row = jnp.moveaxis(energy, 1, 0)
    done = lax.map(lambda item: source(item[0][:, None], item[1][None], item[2][None], item[3][None], ratio, theta)[:, 0],
                   (by_row, wind_speed, wind_dir, ice_mask))
    return jnp.moveaxis(done, 0, 1)
```

```python
import jax
import jax.numpy as jnp
import numpy as np
from jax import lax
from jax.experimental import pallas as pl
from jax.experimental.pallas import tpu as pltpu
from jax.sharding import PartitionSpec as P

NF = 25
ND = 24
NG = 3
ROWS = 4
COLS = 256
LANES = 128
PART = 5 * ND * 8
PER = 5

RATIO = np.float32(1.1) ** np.arange(NF, dtype=np.float32)
THETA = (np.float32(2.0 * np.pi) * np.arange(ND, dtype=np.float32) / np.float32(ND)).astype(np.float32)
COS = np.cos(THETA).astype(np.float32)
SIN = np.sin(THETA).astype(np.float32)
EAST = COS > 0
UP = SIN >= 0
WEIGHT = (RATIO / (np.float32(ND) * RATIO.sum(dtype=np.float32))).astype(np.float32)


def iotas():
    return (
        lax.broadcasted_iota(jnp.int32, (8, LANES), 0),
        lax.broadcasted_iota(jnp.int32, (8, LANES), 1),
    )


def by_sublane(values, sub):
    out = jnp.full((8, LANES), float(values[0]), jnp.float32)
    for j in range(1, 8):
        out = jnp.where(sub == j, float(values[j]), out)
    return out


def direction_tables(sub):
    cu = [by_sublane(np.abs(COS[8 * g : 8 * g + 8]), sub) for g in range(NG)]
    cv = [by_sublane(np.abs(SIN[8 * g : 8 * g + 8]), sub) for g in range(NG)]
    return cu, cv


def east_mask(g, sub):
    if g == 0:
        return sub < 6
    if g == 2:
        return sub >= 2
    return None


def roll(x, shift, axis=1):
    size = x.shape[axis]
    if isinstance(shift, int):
        shift = shift % size
        if shift == 0:
            return x
    return pltpu.roll(x, shift, axis)


def upwind_x(e, edge, sub, lane):
    first, last = lane == 0, lane == LANES - 1
    low, mid, high = e
    both = [jnp.where(sub < 2, high[c], low[c]) for c in (0, 1)]
    both_edge = jnp.where(sub < 2, edge[2], edge[0])

    def from_east(v, beside):
        l0, l1 = roll(v[0], -1), roll(v[1], -1)
        return jnp.where(last, l1, l0), jnp.where(last, beside, l1)

    def from_west(v, beside):
        r0, r1 = roll(v[0], 1), roll(v[1], 1)
        return jnp.where(first, beside, r0), jnp.where(first, r0, r1)

    be, me = from_east(both, both_edge), from_east(mid, edge[1])
    lw, hw = from_west(low, edge[0]), from_west(high, edge[2])
    return [
        [jnp.where(sub < 6, lw[c], be[c]) for c in (0, 1)],
        list(me),
        [jnp.where(sub < 2, be[c], hw[c]) for c in (0, 1)],
    ]


def upwind_y(rows, r, g, sub):
    low = rows[r - 1] if r > 0 else None
    high = rows[r + 1] if r < ROWS - 1 else None
    if g == 0:
        return low
    if g == 2:
        return high
    zero = jnp.zeros((8, LANES), jnp.float32)
    return jnp.where(sub < 4, zero if low is None else low, zero if high is None else high)


def comp_rows(i, g, r, c):
    return pl.ds((i * ND + g * 8) * 8 + c * ROWS + r, 8, 8)


def packed_plus(sub, lane):
    group = (lane // 8) % NG
    d = group * 8 + sub
    return (d < 6) | (d >= 18)


def spread(x, lane):
    x = jnp.where(lane < 8, x, 0.0)
    for step in (8, 16, 32, 64):
        x = x + roll(x, step)
    return x


def edges_kernel(spec_hbm, sea_hbm, x_out, spec, sea, sems):
    sub, lane = iotas()

    def fetch(block):
        part = pl.ds(pl.multiple_of(block * PART, PART), PART)
        return pltpu.make_async_copy(spec_hbm.at[part], spec.at[part], sems.at[block])

    for block in range(NF // PER):
        fetch(block).start()
    sea_copy = pltpu.make_async_copy(sea_hbm, sea, sems.at[NF // PER])
    sea_copy.start()
    here = lane // 2
    shifted = ((lane + 2) & (LANES - 1)) // 2
    plus_at = packed_plus(sub, lane)

    def freqs(block, carry):
        fetch(block).wait()
        easts = wests = jnp.zeros((8, LANES), jnp.float32)
        for t in range(PER):
            i = block * PER + t
            for g in range(NG):
                plus = east_mask(g, sub)
                for r in range(ROWS):
                    v = spec[comp_rows(i, g, r, 0), :]
                    if plus is not None:
                        v = jnp.where(plus, spec[comp_rows(i, g, r, 1), :], v)
                    place = 4 * (NG * t + g) + r
                    v = roll(v, 2 * place)
                    wests = jnp.where(here == place, v, wests)
                    if plus is not None:
                        easts = jnp.where(shifted == place, v, easts)
        x_out[block] = jnp.where(plus_at, roll(easts, 2), wests)
        return carry

    lax.fori_loop(0, NF // PER, freqs, 0)
    sea_copy.wait()
    seaf = sea[...].astype(jnp.float32)
    slot_e = jnp.zeros((8, LANES), jnp.float32)
    slot_w = jnp.zeros((8, LANES), jnp.float32)
    for r in range(ROWS):
        last = jnp.broadcast_to(roll(seaf, 1)[ROWS + r : ROWS + r + 1, 0:1], (8, LANES))
        first = jnp.broadcast_to(seaf[r : r + 1, 0:1], (8, LANES))
        here = (lane == 2 * r) | (lane == 2 * r + 1)
        slot_e = jnp.where(here, last, slot_e)
        slot_w = jnp.where(here, first, slot_w)
    x_out[PER] = spread(slot_e, lane)
    x_out[PER + 1] = spread(slot_w, lane)


def rows_kernel(spec, odd_ref, z_out, a_out):
    sub, _ = iotas()
    odd = odd_ref[0] == 1
    half = sub < 4

    def freqs(block, carry):
        for t in range(PER):
            i = block * PER + t
            load = lambda g, r, c: spec[comp_rows(i, g, r, c), :]
            ups = [load(0, 3, 0), load(0, 3, 1), load(0, 2, 0), load(0, 2, 1)]
            ups += [jnp.where(half, load(1, 3, c), roll(load(1, 2, c), 4, 0)) for c in (0, 1)]
            downs = [load(2, 0, 0), load(2, 0, 1), load(2, 1, 0), load(2, 1, 1)]
            downs += [jnp.where(half, roll(load(1, 1, c), 4, 0), load(1, 0, c)) for c in (0, 1)]
            for j in range(6):
                z_out[i * 6 + j] = jnp.where(odd, ups[j], downs[j])
                a_out[i * 6 + j] = jnp.where(odd, downs[j], ups[j])
        return carry

    lax.fori_loop(0, NF // PER, freqs, 0)


def copy_rows(src, dst):
    def some(j, carry):
        for t in range(10):
            dst[j * 10 + t] = src[j * 10 + t]
        return carry

    lax.fori_loop(0, NF * 6 // 10, some, 0)


def join_kernel(b_in, c_in, sea, even_ref, rows, out, rows_out):
    sub, lane = iotas()
    plus = packed_plus(sub, lane)
    even = even_ref[0] == 1
    for j in range(PER):
        west = jnp.where(even, c_in[j], b_in[j])
        east = jnp.where(even, b_in[j], c_in[j])
        out[j] = jnp.where(plus, west, east)
    west = jnp.where(even, c_in[PER], b_in[PER])
    east = jnp.where(even, b_in[PER + 1], c_in[PER + 1])
    out[PER] = jnp.where(plus, west, east)
    out[PER + 1] = sea[...].astype(jnp.float32)
    copy_rows(rows, rows_out)
    for j in range(PER + 2):
        rows_out[NF * 6 + j] = out[j]


def append_kernel(rows, joined, out):
    copy_rows(rows, out)
    for j in range(PER + 2):
        out[NF * 6 + j] = joined[j]


def row(x, j):
    return jnp.broadcast_to(x[j : j + 1, :], (8, LANES))


def gain_kernel(ratio_ref, wind_speed, wind_dir, ice, f_out, align):
    sub, lane = iotas()
    icef = ice[...].astype(jnp.float32)
    blow = (1.0 - icef) * 0.05 * wind_speed[...]
    cw, sw = jnp.cos(wind_dir[...]), jnp.sin(wind_dir[...])
    for g in range(NG):
        ct = by_sublane(COS[8 * g : 8 * g + 8], sub)
        st = by_sublane(SIN[8 * g : 8 * g + 8], sub)
        for rc in range(8):
            align[g * 8 + rc] = row(blow, rc) * jnp.maximum(ct * row(cw, rc) + st * row(sw, rc), 0.0)

    def freqs(block, carry):
        for t in range(PER):
            i = block * PER + t
            ratio = ratio_ref[i]
            for rc in range(8):
                cold = 0.7 * row(icef, rc)
                for g in range(NG):
                    f_out[i * 24 + g * 8 + rc] = jnp.exp(ratio * align[g * 8 + rc] - cold)
        return carry

    lax.fori_loop(0, NF // PER, freqs, 0)


def inner_kernel(spec, courant, ratio_ref, weight_ref, sea, joined, f, pf_out, mom_out, edge2):
    sub, lane = iotas()
    cu, cv = direction_tables(sub)
    seaf = sea[...].astype(jnp.float32)
    slot = lane // 8
    group = slot % NG
    rr = (lane % 8) // 2
    plus = packed_plus(sub, lane)
    up = group * 8 + sub < 12
    cup = jnp.where(group == 0, cu[0], jnp.where(group == 1, cu[1], cu[2]))
    cvp = jnp.where(group == 0, cv[0], jnp.where(group == 1, cv[1], cv[2]))
    sea_edge = joined[PER]
    for j in range(PER):
        co = jnp.zeros((8, LANES), jnp.float32)
        for t in range(PER):
            co = jnp.where(slot // NG == t, courant[j * PER + t], co)
        au, av = co * cup, co * cvp
        m = joined[j]
        mx = jnp.where(plus, roll(m, 1), roll(m, -1))
        my = jnp.where(up, jnp.where(rr >= 1, roll(m, 2), 0.0), jnp.where(rr <= 2, roll(m, -2), 0.0))
        edge2[j] = sea_edge * ((1.0 - au - av) * m + au * mx + av * my)

    def freqs(block, mom):
        mom = list(mom)
        m1 = joined[block]
        m2 = edge2[block]
        for t in range(PER):
            i = block * PER + t
            ci = courant[i]
            ratio = ratio_ref[i]
            weight = weight_ref[i]
            total = [None] * 8
            au, av = [ci * x for x in cu], [ci * x for x in cv]
            a0 = [1.0 - x - y for x, y in zip(au, av)]
            e = [[[spec[comp_rows(i, g, r, c), :] for c in (0, 1)] for r in range(ROWS)] for g in range(NG)]
            for m in (m1, m2):
                new = [[[None, None] for _ in range(ROWS)] for _ in range(NG)]
                for r in range(ROWS):
                    edge = [roll(m, -(8 * (NG * t + g) + 2 * r + 1)) for g in range(NG)]
                    xs = upwind_x([e[g][r] for g in range(NG)], edge, sub, lane)
                    for g in range(NG):
                        for c in (0, 1):
                            val = a0[g] * e[g][r][c] + au[g] * xs[g][c]
                            y = upwind_y([e[g][q][c] for q in range(ROWS)], r, g, sub)
                            if y is not None:
                                val = val + av[g] * y
                            new[g][r][c] = val * row(seaf, c * ROWS + r)
                e = new
            for g in range(NG):
                for r in range(ROWS):
                    for c in (0, 1):
                        rc = c * ROWS + r
                        at = i * 24 + g * 8 + rc
                        total[rc] = e[g][r][c] if total[rc] is None else total[rc] + e[g][r][c]
                        pf_out[at] = e[g][r][c] * f[at]
            for rc in range(8):
                wt = weight * total[rc]
                mom[rc] = mom[rc] + wt
                mom[8 + rc] = mom[8 + rc] + wt * ratio
        return tuple(mom)

    mom = lax.fori_loop(0, NF // PER, freqs, (jnp.zeros((8, LANES), jnp.float32),) * 16)
    for j in range(16):
        mom_out[j] = mom[j]


def outer_kernel(courant, ratio_ref, weight_ref, odd_ref, pf, f, mom, z_in, a_in, joined, out_hbm, fixed, growth, out, sems):
    sub, lane = iotas()
    cu, cv = direction_tables(sub)
    odd = odd_ref[0] == 1
    half = sub < 4
    tail = NF * 6
    zsea = jnp.where(odd, a_in[tail + PER + 1], z_in[tail + PER + 1])
    hsea = jnp.where(odd, z_in[tail + PER + 1], a_in[tail + PER + 1])
    sea = joined[PER + 1]
    sea_edge = joined[PER]
    sides = []
    for first, second, beside, at in ((0, 1, zsea, 3), (3, 2, hsea, 0)):
        edge = [roll(sea_edge, -(8 * g + 2 * first + 1)) for g in range(NG)]
        s0 = [row(sea, c * ROWS + first) for c in (0, 1)]
        s1 = [row(sea, c * ROWS + second) for c in (0, 1)]
        sm = [row(beside, c * ROWS + at) for c in (0, 1)]
        sw = upwind_x([s0] * NG, edge, sub, lane)
        sides.append([[(s0[c] * (s0[c] + sm[c]), s0[c] * (sw[g][c] + sm[c]), s0[c] * sm[c], s1[c] * s0[c]) for c in (0, 1)] for g in range(NG)])
    mixed = [tuple(jnp.where(half, x, y) for x, y in zip(sides[0][1][c], sides[1][1][c])) for c in (0, 1)]
    masks = [sides[0][0], mixed, sides[1][2]]

    def fix(block, moms):
        moms = list(moms)
        below = roll(jnp.where(odd, a_in[tail + block], z_in[tail + block]), -6)
        above = jnp.where(odd, z_in[tail + block], a_in[tail + block])
        corner = [below, jnp.where(half, below, above), above]
        for t in range(PER):
            i = block * PER + t
            ci = courant[i]
            ratio = ratio_ref[i]
            weight = weight_ref[i]
            zs = [z_in[i * 6 + j] for j in range(6)]
            as_ = [a_in[i * 6 + j] for j in range(6)]
            us = [jnp.where(odd, x, y) for x, y in zip(as_, zs)]
            ds = [jnp.where(odd, y, x) for x, y in zip(as_, zs)]
            total = {}
            h1 = [us[0:2], [jnp.where(half, us[4 + c], ds[4 + c]) for c in (0, 1)], ds[0:2]]
            h2 = [us[2:4], [roll(jnp.where(half, ds[4 + c], us[4 + c]), 4, 0) for c in (0, 1)], ds[2:4]]
            hw = upwind_x(h1, [roll(corner[g], -(8 * (NG * t + g) + 1)) for g in range(NG)], sub, lane)
            for g in range(NG):
                au, av = ci * cu[g], ci * cv[g]
                a0 = 1.0 - au - av
                k1, k2, k3 = a0 * av, au * av, av * av
                for c in (0, 1):
                    t1, t2, t3, t4 = masks[g][c]
                    first = k1 * h1[g][c] * t1 + k2 * hw[g][c] * t2 + k3 * h2[g][c] * t3
                    second = k3 * h1[g][c] * t4
                    if g == 1:
                        adds = [(0, jnp.where(half, first, 0.0)), (1, jnp.where(half, second, 0.0)), (3, jnp.where(half, 0.0, first)), (2, jnp.where(half, 0.0, second))]
                    elif g == 0:
                        adds = [(0, first), (1, second)]
                    else:
                        adds = [(3, first), (2, second)]
                    for r, add in adds:
                        rc = c * ROWS + r
                        total[rc] = add if rc not in total else total[rc] + add
                        at = i * 24 + g * 8 + rc
                        fixed[at] = pf[at] + add * f[at]
            for rc in range(8):
                wt = weight * total[rc]
                moms[rc] = moms[rc] + wt
                moms[8 + rc] = moms[8 + rc] + wt * ratio
        return tuple(moms)

    moms = lax.fori_loop(0, NF // PER, fix, tuple(mom[j] for j in range(16)))

    m0 = jnp.zeros((8, LANES), jnp.float32)
    m1 = jnp.zeros((8, LANES), jnp.float32)
    for rc in range(8):
        m0 = jnp.where(sub == rc, jnp.sum(moms[rc], axis=0, keepdims=True), m0)
        m1 = jnp.where(sub == rc, jnp.sum(moms[8 + rc], axis=0, keepdims=True), m1)
    loss = 0.02 * (m1 / jnp.maximum(m0, 0.05))
    for i in range(NF):
        growth[i] = jnp.exp(-float(RATIO[i]) * loss)

    def send(block):
        part = pl.ds(pl.multiple_of(block * PART, PART), PART)
        return pltpu.make_async_copy(out.at[part], out_hbm.at[part], sems.at[block])

    def grow(block, carry):
        for t in range(PER):
            i = block * PER + t
            for rc in range(8):
                factor = jnp.broadcast_to(growth[i, rc : rc + 1, :], (8, LANES))
                for g in range(NG):
                    at = i * 24 + g * 8 + rc
                    r = rc % ROWS
                    touched = g == 1 or (g == 0 and r < 2) or (g == 2 and r >= 2)
                    val = fixed[at] if touched else pf[at]
                    out[comp_rows(i, g, r, rc // ROWS), :] = val * factor
        send(block).start()
        return carry

    lax.fori_loop(0, NF // PER, grow, 0)
    for block in range(NF // PER):
        send(block).wait()


VM = pl.BlockSpec(memory_space=pltpu.VMEM)
SM = pl.BlockSpec(memory_space=pltpu.SMEM)
HBM = pl.BlockSpec(memory_space=pltpu.HBM)


def REG(n):
    return jax.ShapeDtypeStruct((n, 8, LANES), jnp.float32)


def call(kernel, outs, ins, scratch=(), vmem=24 << 20, outspecs=None, cost=1.0):
    return pl.pallas_call(
        kernel,
        out_shape=outs,
        in_specs=ins,
        out_specs=jax.tree.map(lambda _: VM, outs) if outspecs is None else outspecs,
        scratch_shapes=list(scratch),
        compiler_params=pltpu.CompilerParams(vmem_limit_bytes=vmem),
        cost_estimate=pl.CostEstimate(flops=0, bytes_accessed=int(cost * 3.6e6), transcendentals=0),
    )


def tiles(x):
    lead = x.shape[:-2]
    x = x.reshape(lead + (ROWS, 2, LANES))
    return jnp.swapaxes(x, -3, -2).reshape(lead + (8, LANES))


def untiles(x):
    lead = x.shape[:-2]
    x = jnp.swapaxes(x.reshape(lead + (2, ROWS, LANES)), -3, -2)
    return x.reshape(lead + (ROWS, COLS))


def on_device(spectra, courant, wind_speed, wind_dir, sea_mask, ice_mask):
    ns, nq = lax.axis_size("strip"), lax.axis_size("pt")
    pair_a = [(i, i ^ 1) for i in range(ns)]
    pair_z = [(i, ((i + 1) ^ 1) - 1) for i in range(1, ns - 1)]
    pair_b = [(i, i ^ 1) for i in range(nq)]
    pair_c = [(i, (((i + 1) ^ 1) - 1) % nq) for i in range(nq)]
    odd = (lax.axis_index("strip") % 2).reshape(1).astype(jnp.int32)
    even = (1 - lax.axis_index("pt") % 2).reshape(1).astype(jnp.int32)
    ratio, weight = jnp.asarray(RATIO), jnp.asarray(WEIGHT)
    spec = tiles(spectra).reshape(NF * ND * 8, LANES)
    wind_speed, wind_dir, sea, ice = (tiles(x) for x in (wind_speed, wind_dir, sea_mask, ice_mask))
    part_sems = pltpu.SemaphoreType.DMA((NF // PER + 1,))
    whole = pltpu.VMEM((NF * ND * 8, LANES), jnp.float32)
    xmsg = call(edges_kernel, REG(PER + 2), [HBM, HBM], [whole, pltpu.VMEM((8, LANES), jnp.int32), part_sems], cost=2.0, vmem=62 << 20)(spec, sea)
    cin = lax.ppermute(xmsg, "pt", pair_c)
    bin_ = lax.ppermute(xmsg, "pt", pair_b)
    zrows, arows = call(rows_kernel, (REG(NF * 6), REG(NF * 6)), [VM, SM], cost=0.7)(spec, odd)
    f = call(gain_kernel, REG(NF * 24), [SM, VM, VM, VM], [pltpu.VMEM((24, 8, LANES), jnp.float32)], cost=1.0)(
        ratio, wind_speed, wind_dir, ice
    )
    zrows, f = lax.optimization_barrier((zrows, f))
    joined, zmsg = call(join_kernel, (REG(PER + 2), REG(NF * 6 + PER + 2)), [VM, VM, VM, SM, VM], cost=0.2)(bin_, cin, sea, even, zrows)
    zin = lax.ppermute(zmsg, "strip", pair_z)
    pf, mom = call(
        inner_kernel,
        (REG(NF * 24), REG(16)),
        [VM, SM, SM, SM, VM, VM, VM],
        [pltpu.VMEM((PER, 8, LANES), jnp.float32)],
        cost=5.0,
    )(spec, courant, ratio, weight, sea, joined, f)
    arows, mom = lax.optimization_barrier((arows, mom))
    amsg = call(append_kernel, REG(NF * 6 + PER + 2), [VM, VM], cost=0.2)(arows, joined)
    ain = lax.ppermute(amsg, "strip", pair_a)
    out = call(
        outer_kernel,
        jax.ShapeDtypeStruct((NF * ND * 8, LANES), jnp.float32),
        [SM, SM, SM, SM, VM, VM, VM, VM, VM, VM],
        [pltpu.VMEM((NF * 24, 8, LANES), jnp.float32), pltpu.VMEM((NF, 8, LANES), jnp.float32), whole, part_sems],
        outspecs=HBM,
        cost=3.0,
    )(courant, ratio, weight, odd, pf, f, mom, zin, ain, joined)
    return untiles(out.reshape(NF * ND, 8, LANES))


def solution(mesh):
    in_specs = (
        P(None, "strip", "pt"),
        P(),
        P("strip", "pt"),
        P("strip", "pt"),
        P("strip", "pt"),
        P("strip", "pt"),
    )
    return jax.shard_map(
        on_device, mesh=mesh, in_specs=in_specs, out_specs=P(None, "strip", "pt"), check_vma=False
    )
```

```python
import jax
import jax.numpy as jnp
import numpy as np
from jax import lax
from jax.experimental import pallas as pl
from jax.experimental.pallas import tpu as pltpu
from jax.sharding import PartitionSpec as P

NF = 25
ND = 24
NG = 3
ROWS = 4
COLS = 256
LANES = 128
PART = 5 * ND * 8
PAD = 1
PER = 5

RATIO = np.float32(1.1) ** np.arange(NF, dtype=np.float32)
THETA = (np.float32(2.0 * np.pi) * np.arange(ND, dtype=np.float32) / np.float32(ND)).astype(np.float32)
COS = np.cos(THETA).astype(np.float32)
SIN = np.sin(THETA).astype(np.float32)
EAST = COS > 0
UP = SIN >= 0
WEIGHT = (RATIO / (np.float32(ND) * RATIO.sum(dtype=np.float32))).astype(np.float32)


def iotas():
    return (
        lax.broadcasted_iota(jnp.int32, (8, LANES), 0),
        lax.broadcasted_iota(jnp.int32, (8, LANES), 1),
    )


def by_sublane(values, sub):
    out = jnp.full((8, LANES), float(values[0]), jnp.float32)
    for j in range(1, 8):
        out = jnp.where(sub == j, float(values[j]), out)
    return out


def direction_tables(sub):
    cu = [by_sublane(np.abs(COS[8 * g : 8 * g + 8]), sub) for g in range(NG)]
    cv = [by_sublane(np.abs(SIN[8 * g : 8 * g + 8]), sub) for g in range(NG)]
    return cu, cv


def east_mask(g, sub):
    if g == 0:
        return sub < 6
    if g == 2:
        return sub >= 2
    return None


def roll(x, shift, axis=1):
    size = x.shape[axis]
    if isinstance(shift, int):
        shift = shift % size
        if shift == 0:
            return x
    return pltpu.roll(x, shift, axis)


def upwind_x(e, edge, sub, lane):
    first, last = lane == 0, lane == LANES - 1
    low, mid, high = e
    both = [jnp.where(sub < 2, high[c], low[c]) for c in (0, 1)]
    both_edge = jnp.where(sub < 2, edge[2], edge[0])

    def from_east(v, beside):
        l0, l1 = roll(v[0], -1), roll(v[1], -1)
        return jnp.where(last, l1, l0), jnp.where(last, beside, l1)

    def from_west(v, beside):
        r0, r1 = roll(v[0], 1), roll(v[1], 1)
        return jnp.where(first, beside, r0), jnp.where(first, r0, r1)

    be, me = from_east(both, both_edge), from_east(mid, edge[1])
    lw, hw = from_west(low, edge[0]), from_west(high, edge[2])
    return [
        [jnp.where(sub < 6, lw[c], be[c]) for c in (0, 1)],
        list(me),
        [jnp.where(sub < 2, be[c], hw[c]) for c in (0, 1)],
    ]


def upwind_y(rows, r, g, sub):
    low = rows[r - 1] if r > 0 else None
    high = rows[r + 1] if r < ROWS - 1 else None
    if g == 0:
        return low
    if g == 2:
        return high
    zero = jnp.zeros((8, LANES), jnp.float32)
    return jnp.where(sub < 4, zero if low is None else low, zero if high is None else high)


def comp_rows(i, g, r, c):
    return pl.ds((i * ND + g * 8) * 8 + c * ROWS + r, 8, 8)


def packed_plus(sub, lane):
    group = (lane // 8) % NG
    d = group * 8 + sub
    return (d < 6) | (d >= 18)


def spread(x, lane):
    x = jnp.where(lane < 8, x, 0.0)
    for step in (8, 16, 32, 64):
        x = x + roll(x, step)
    return x


def edges_kernel(spec_hbm, sea_hbm, x_out, spec, sea, sems):
    sub, lane = iotas()

    def fetch(block):
        part = pl.ds(block * PART, PART)
        return pltpu.make_async_copy(spec_hbm.at[part], spec.at[part], sems.at[block])

    sea_copy = pltpu.make_async_copy(sea_hbm, sea, sems.at[NF // PER])
    sea_copy.start()
    for block in range(NF // PER):
        fetch(block).start()
    here = lane // 2
    shifted = ((lane + 2) & (LANES - 1)) // 2
    plus_at = packed_plus(sub, lane)

    sea_copy.wait()
    seaf = sea[...].astype(jnp.float32)
    slot_e = jnp.zeros((8, LANES), jnp.float32)
    slot_w = jnp.zeros((8, LANES), jnp.float32)
    for r in range(ROWS):
        last = jnp.broadcast_to(roll(seaf, 1)[ROWS + r : ROWS + r + 1, 0:1], (8, LANES))
        first = jnp.broadcast_to(seaf[r : r + 1, 0:1], (8, LANES))
        place = lane // 2 == r
        slot_e = jnp.where(place, last, slot_e)
        slot_w = jnp.where(place, first, slot_w)
    x_out[PER] = spread(slot_e, lane)
    x_out[PER + 1] = spread(slot_w, lane)

    for block in range(NF // PER):
        fetch(block).wait()
        zero = jnp.zeros((8, LANES), jnp.float32)
        easts, wests = [zero] * 3, [zero] * 3
        for t in range(PER):
            i = block * PER + t
            for g in range(NG):
                plus = east_mask(g, sub)
                for r in range(ROWS):
                    v = spec[comp_rows(i, g, r, 0), :]
                    if plus is not None:
                        v = jnp.where(plus, spec[comp_rows(i, g, r, 1), :], v)
                    place = 4 * (NG * t + g) + r
                    v = roll(v, 2 * place)
                    wests[g] = jnp.where(here == place, v, wests[g])
                    if plus is not None:
                        easts[g] = jnp.where(shifted == place, v, easts[g])
        x_out[block] = jnp.where(plus_at, roll(easts[0] + easts[2], 2), wests[0] + wests[1] + wests[2])


def rows_kernel(spec, odd_ref, z_out, a_out):
    sub, _ = iotas()
    odd = odd_ref[0] == 1
    half = sub < 4

    def freqs(block, carry):
        for t in range(PER):
            i = block * PER + t
            load = lambda g, r, c: spec[comp_rows(i, g, r, c), :]
            ups = [load(0, 3, 0), load(0, 3, 1), load(0, 2, 0), load(0, 2, 1)]
            ups += [jnp.where(half, load(1, 3, c), roll(load(1, 2, c), 4, 0)) for c in (0, 1)]
            downs = [load(2, 0, 0), load(2, 0, 1), load(2, 1, 0), load(2, 1, 1)]
            downs += [jnp.where(half, roll(load(1, 1, c), 4, 0), load(1, 0, c)) for c in (0, 1)]
            for j in range(6):
                z_out[i * 6 + j] = jnp.where(odd, ups[j], downs[j])
                a_out[i * 6 + j] = jnp.where(odd, downs[j], ups[j])
        return carry

    lax.fori_loop(0, NF // PER, freqs, 0)


def blocks(body, carry):
    for block in range(NF // PER):
        carry = body(block, carry)
    return carry


def copy_rows(src, dst):
    def some(j, carry):
        for t in range(10):
            dst[j * 10 + t] = src[j * 10 + t]
        return carry

    lax.fori_loop(0, NF * 6 // 10, some, 0)


def join_kernel(b_in, c_in, sea, even_ref, rows, out, rows_out):
    sub, lane = iotas()
    plus = packed_plus(sub, lane)
    even = even_ref[0] == 1
    for j in range(PER):
        west = jnp.where(even, c_in[j], b_in[j])
        east = jnp.where(even, b_in[j], c_in[j])
        out[j] = jnp.where(plus, west, east)
    west = jnp.where(even, c_in[PER], b_in[PER])
    east = jnp.where(even, b_in[PER + 1], c_in[PER + 1])
    out[PER] = jnp.where(plus, west, east)
    out[PER + 1] = sea[...].astype(jnp.float32)
    copy_rows(rows, rows_out)
    for j in range(PER):
        rows_out[NF * 6 + j] = out[j]
    rows_out[NF * 6 + PER] = out[PER + 1]
    for j in range(PER + 1, PER + 1 + PAD):
        rows_out[NF * 6 + j] = out[PER]


def append_kernel(rows, joined, out):
    copy_rows(rows, out)
    for j in range(PER):
        out[NF * 6 + j] = joined[j]
    out[NF * 6 + PER] = joined[PER + 1]


def row(x, j):
    return jnp.broadcast_to(x[j : j + 1, :], (8, LANES))


def gain_kernel(ratio_ref, wind_speed, wind_dir, ice, e_in, f_out, fe_out, align):
    sub, lane = iotas()
    icef = ice[...].astype(jnp.float32)
    blow = (1.0 - icef) * 0.05 * wind_speed[...]
    cw, sw = jnp.cos(wind_dir[...]), jnp.sin(wind_dir[...])
    for g in range(NG):
        ct = by_sublane(COS[8 * g : 8 * g + 8], sub)
        st = by_sublane(SIN[8 * g : 8 * g + 8], sub)
        for rc in range(8):
            align[g * 8 + rc] = row(blow, rc) * jnp.maximum(ct * row(cw, rc) + st * row(sw, rc), 0.0)

    def freqs(block, carry):
        for t in range(PER):
            i = block * PER + t
            ratio = ratio_ref[i]
            for rc in range(8):
                cold = 0.7 * row(icef, rc)
                for g in range(NG):
                    at = i * 24 + g * 8 + rc
                    value = jnp.exp(ratio * align[g * 8 + rc] - cold)
                    fe_out[at] = value * e_in[at]
                    r = rc % ROWS
                    if g == 1 or (g == 0) == (r < 2):
                        f_out[at] = value
        return carry

    lax.fori_loop(0, NF // PER, freqs, 0)


def inner_kernel(spec, courant, sea, joined, e_out, mom_out, edge2):
    sub, lane = iotas()
    cu, cv = direction_tables(sub)
    seaf = sea[...].astype(jnp.float32)
    slot = lane // 8
    group = slot % NG
    rr = (lane % 8) // 2
    plus = packed_plus(sub, lane)
    up = group * 8 + sub < 12
    cup = jnp.where(group == 0, cu[0], jnp.where(group == 1, cu[1], cu[2]))
    cvp = jnp.where(group == 0, cv[0], jnp.where(group == 1, cv[1], cv[2]))
    sea_edge = joined[PER]
    for j in range(PER):
        co = jnp.zeros((8, LANES), jnp.float32)
        for t in range(PER):
            co = jnp.where(slot // NG == t, courant[j * PER + t], co)
        au, av = co * cup, co * cvp
        m = joined[j]
        mx = jnp.where(plus, roll(m, 1), roll(m, -1))
        my = jnp.where(up, jnp.where(rr >= 1, roll(m, 2), 0.0), jnp.where(rr <= 2, roll(m, -2), 0.0))
        edge2[j] = sea_edge * ((1.0 - au - av) * m + au * mx + av * my)

    def freqs(block, mom):
        mom = list(mom)
        m1 = joined[block]
        m2 = edge2[block]
        waiting = None

        def put(i, e):
            for g in range(NG):
                for r in range(ROWS):
                    for c in (0, 1):
                        e_out[i * 24 + g * 8 + c * ROWS + r] = e[g][r][c]

        for t in range(PER):
            i = block * PER + t
            ci = courant[i]
            ratio, weight = float(RATIO[i]), float(WEIGHT[i])
            au, av = [ci * x for x in cu], [ci * x for x in cv]
            a0 = [1.0 - x - y for x, y in zip(au, av)]
            e = [[[spec[comp_rows(i, g, r, c), :] for c in (0, 1)] for r in range(ROWS)] for g in range(NG)]
            if waiting is not None:
                put(*waiting)
            for m in (m1, m2):
                new = [[[None, None] for _ in range(ROWS)] for _ in range(NG)]
                for r in range(ROWS):
                    edge = [roll(m, -(8 * (NG * t + g) + 2 * r + 1)) for g in range(NG)]
                    xs = upwind_x([e[g][r] for g in range(NG)], edge, sub, lane)
                    for g in range(NG):
                        for c in (0, 1):
                            val = a0[g] * e[g][r][c] + au[g] * xs[g][c]
                            y = upwind_y([e[g][q][c] for q in range(ROWS)], r, g, sub)
                            if y is not None:
                                val = val + av[g] * y
                            new[g][r][c] = val * row(seaf, c * ROWS + r)
                e = new
            for r in range(ROWS):
                for c in (0, 1):
                    rc = c * ROWS + r
                    wt = weight * (e[0][r][c] + e[1][r][c] + e[2][r][c])
                    mom[rc] = mom[rc] + wt
                    mom[8 + rc] = mom[8 + rc] + wt * ratio
            waiting = (i, e)
        put(*waiting)
        return tuple(mom)

    mom = blocks(freqs, (jnp.zeros((8, LANES), jnp.float32),) * 16)
    for j in range(16):
        mom_out[j] = mom[j]


def side(up, courant, f, msg, joined, fixed, moms, store):
    sub, lane = iotas()
    cu, cv = direction_tables(sub)
    mine = sub < 4 if up else sub >= 4
    first, second, at = (0, 1, 3) if up else (3, 2, 0)
    main = 0 if up else 2
    tail = NF * 6
    sea, sea_edge, beside = joined[PER + 1], joined[PER], msg[tail + PER]
    edge = [roll(sea_edge, -(8 * g + 2 * first + 1)) for g in range(NG)]
    s0 = [row(sea, c * ROWS + first) for c in (0, 1)]
    s1 = [row(sea, c * ROWS + second) for c in (0, 1)]
    sm = [row(beside, c * ROWS + at) for c in (0, 1)]
    masks = {}
    for g in (main, 1):
        sw = upwind_one(s0, edge[g], g, sub, lane)
        masks[g] = [(s0[c] * (s0[c] + sm[c]), s0[c] * (sw[c] + sm[c]), s0[c] * sm[c], s1[c] * s0[c]) for c in (0, 1)]
    masks[1] = [tuple(jnp.where(mine, x, 0.0) for x in masks[1][c]) for c in (0, 1)]

    corners = [roll(msg[tail + block], -(2 * at + 1)) for block in range(NF // PER)]

    def freqs(block, carry):
        moms = list(carry)
        corner = corners[block]
        waiting = []

        def put():
            for where, value in waiting.pop(0):
                fixed[where] = value

        for t in range(PER):
            i = block * PER + t
            ci = courant[i]
            ratio, weight = float(RATIO[i]), float(WEIGHT[i])
            m = [msg[i * 6 + j] for j in range(6)]
            fs = [[[f[i * 24 + g * 8 + c * ROWS + r] for c in (0, 1)] for r in (first, second)] for g in (main, 1)]
            if len(waiting) == 2:
                put()
            total = [[None, None], [None, None]]
            results = []
            for slot, g in enumerate((main, 1)):
                h1 = m[0:2] if slot == 0 else m[4:6]
                h2 = m[2:4] if slot == 0 else [roll(v, 4, 0) for v in m[4:6]]
                hw = upwind_one(h1, roll(corner, -8 * (NG * t + g)), g, sub, lane)
                au, av = ci * cu[g], ci * cv[g]
                a0 = 1.0 - au - av
                k1, k2, k3 = a0 * av, au * av, av * av
                for c in (0, 1):
                    t1, t2, t3, t4 = masks[g][c]
                    adds = (k1 * h1[c] * t1 + k2 * hw[c] * t2 + k3 * h2[c] * t3, k3 * h1[c] * t4)
                    for n, add in enumerate(adds):
                        total[n][c] = add if total[n][c] is None else total[n][c] + add
                        results.append((i * 8 + slot * 4 + n * 2 + c, add * fs[slot][n][c]))
            for n in (0, 1):
                for c in (0, 1):
                    wt = weight * total[n][c]
                    j = n * 2 + c
                    moms[j] = moms[j] + wt
                    moms[4 + j] = moms[4 + j] + wt * ratio
            waiting.append(results)
        while waiting:
            put()
        return tuple(moms)

    rcs = [c * ROWS + r for r in (first, second) for c in (0, 1)]
    start = tuple(moms[rc] for rc in rcs) + tuple(moms[8 + rc] for rc in rcs)
    done = blocks(freqs, start)
    for rc in range(8):
        if rc not in rcs:
            store[rc] = moms[rc]
            store[8 + rc] = moms[8 + rc]
    for j, rc in enumerate(rcs):
        store[rc] = done[j]
        store[8 + rc] = done[4 + j]


def upwind_one(e, edge, g, sub, lane):
    first, last = lane == 0, lane == LANES - 1
    l0, l1 = roll(e[0], -1), roll(e[1], -1)
    x0, x1 = jnp.where(last, l1, l0), jnp.where(last, edge, l1)
    plus = east_mask(g, sub)
    if plus is None:
        return x0, x1
    r0, r1 = roll(e[0], 1), roll(e[1], 1)
    w0, w1 = jnp.where(first, edge, r0), jnp.where(first, r0, r1)
    return jnp.where(plus, w0, x0), jnp.where(plus, w1, x1)


def near_kernel(courant, odd_ref, f, mom, a_in, joined, fixed, mom_out):
    for up in (True, False):

        @pl.when(odd_ref[0] == (1 if up else 0))
        def _():
            side(up, courant, f, a_in, joined, fixed, mom, mom_out)


def outer_kernel(courant, odd_ref, pf, f, mom, near, z_in, joined, out_hbm, far, mom2, growth, out, sems):
    sub, _ = iotas()
    odd = odd_ref[0] == 1
    for up in (True, False):

        @pl.when(odd_ref[0] == (0 if up else 1))
        def _():
            side(up, courant, f, z_in, joined, far, mom, mom2)

    m0 = jnp.zeros((8, LANES), jnp.float32)
    m1 = jnp.zeros((8, LANES), jnp.float32)
    for rc in range(8):
        m0 = jnp.where(sub == rc, jnp.sum(mom2[rc], axis=0, keepdims=True), m0)
        m1 = jnp.where(sub == rc, jnp.sum(mom2[8 + rc], axis=0, keepdims=True), m1)
    loss = 0.02 * (m1 / jnp.maximum(m0, 0.05))
    for i in range(NF):
        growth[i] = jnp.exp(-float(RATIO[i]) * loss)

    def send(block):
        part = pl.ds(pl.multiple_of(block * PART, PART), PART)
        return pltpu.make_async_copy(out.at[part], out_hbm.at[part], sems.at[block])

    def grow(block, carry):
        for t in range(PER):
            i = block * PER + t
            a = [near[i * 8 + j] for j in range(8)]
            z = [far[i * 8 + j] for j in range(8)]
            ups = [jnp.where(odd, x, y) for x, y in zip(a, z)]
            downs = [jnp.where(odd, y, x) for x, y in zip(a, z)]
            for rc in range(8):
                c, r = rc // ROWS, rc % ROWS
                factor = jnp.broadcast_to(growth[i, rc : rc + 1, :], (8, LANES))
                for g in range(NG):
                    val = pf[i * 24 + g * 8 + rc]
                    if r < 2 and g < 2:
                        val = val + ups[(0 if g == 0 else 4) + r * 2 + c]
                    if r >= 2 and g > 0:
                        val = val + downs[(0 if g == 2 else 4) + (3 - r) * 2 + c]
                    out[comp_rows(i, g, r, c), :] = val * factor
        send(block).start()
        return carry

    lax.fori_loop(0, NF // PER, grow, 0)
    for block in range(NF // PER):
        send(block).wait()


VM = pl.BlockSpec(memory_space=pltpu.VMEM)
SM = pl.BlockSpec(memory_space=pltpu.SMEM)
HBM = pl.BlockSpec(memory_space=pltpu.HBM)


def REG(n):
    return jax.ShapeDtypeStruct((n, 8, LANES), jnp.float32)


def call(kernel, outs, ins, scratch=(), vmem=24 << 20, outspecs=None, cost=1.0):
    return pl.pallas_call(
        kernel,
        out_shape=outs,
        in_specs=ins,
        out_specs=jax.tree.map(lambda _: VM, outs) if outspecs is None else outspecs,
        scratch_shapes=list(scratch),
        compiler_params=pltpu.CompilerParams(vmem_limit_bytes=vmem),
        cost_estimate=pl.CostEstimate(flops=0, bytes_accessed=int(cost * 3.6e6), transcendentals=0),
    )


def tiles(x):
    lead = x.shape[:-2]
    x = x.reshape(lead + (ROWS, 2, LANES))
    return jnp.swapaxes(x, -3, -2).reshape(lead + (8, LANES))


def untiles(x):
    lead = x.shape[:-2]
    x = jnp.swapaxes(x.reshape(lead + (2, ROWS, LANES)), -3, -2)
    return x.reshape(lead + (ROWS, COLS))


def on_device(spectra, courant, wind_speed, wind_dir, sea_mask, ice_mask):
    ns, nq = lax.axis_size("strip"), lax.axis_size("pt")
    pair_a = [(i, i ^ 1) for i in range(ns)]
    pair_z = [(i, ((i + 1) ^ 1) - 1) for i in range(1, ns - 1)]
    pair_b = [(i, i ^ 1) for i in range(nq)]
    pair_c = [(i, (((i + 1) ^ 1) - 1) % nq) for i in range(nq)]
    odd = (lax.axis_index("strip") % 2).reshape(1).astype(jnp.int32)
    even = (1 - lax.axis_index("pt") % 2).reshape(1).astype(jnp.int32)
    ratio = jnp.asarray(RATIO)
    spec = tiles(spectra).reshape(NF * ND * 8, LANES)
    wind_speed, wind_dir, sea, ice = (tiles(x) for x in (wind_speed, wind_dir, sea_mask, ice_mask))
    part_sems = pltpu.SemaphoreType.DMA((NF // PER + 1,))
    whole = pltpu.VMEM((NF * ND * 8, LANES), jnp.float32)
    xmsg = call(edges_kernel, REG(PER + 2), [HBM, HBM], [whole, pltpu.VMEM((8, LANES), jnp.int32), part_sems], cost=2.0, vmem=62 << 20)(spec, sea)
    bin_ = lax.ppermute(xmsg, "pt", pair_b)
    cin = lax.ppermute(xmsg, "pt", pair_c)
    zrows, arows = call(rows_kernel, (REG(NF * 6), REG(NF * 6)), [VM, SM], cost=0.7)(spec, odd)
    joined, zmsg = call(join_kernel, (REG(PER + 2), REG(NF * 6 + PER + 1 + PAD)), [VM, VM, VM, SM, VM], cost=0.2)(bin_, cin, sea, even, zrows)
    zin = lax.ppermute(zmsg, "strip", pair_z)
    e2, mom = call(
        inner_kernel,
        (REG(NF * 24), REG(16)),
        [VM, SM, VM, VM],
        [pltpu.VMEM((PER, 8, LANES), jnp.float32)],
        cost=5.0,
    )(spec, courant, sea, joined)
    amsg = call(append_kernel, REG(NF * 6 + PER + 1), [VM, VM], cost=0.2)(arows, joined)
    ain = lax.ppermute(amsg, "strip", pair_a)
    ratio, _ = lax.optimization_barrier((ratio, amsg))
    f, fe = call(gain_kernel, (REG(NF * 24), REG(NF * 24)), [SM, VM, VM, VM, VM], [pltpu.VMEM((24, 8, LANES), jnp.float32)], cost=1.0)(
        ratio, wind_speed, wind_dir, ice, e2
    )
    near, mom = call(near_kernel, (REG(NF * 8), REG(16)), [SM, SM, VM, VM, VM, VM], cost=0.0)(courant, odd, f, mom, ain, joined)
    out = call(
        outer_kernel,
        jax.ShapeDtypeStruct((NF * ND * 8, LANES), jnp.float32),
        [SM, SM, VM, VM, VM, VM, VM, VM],
        [
            pltpu.VMEM((NF * 8, 8, LANES), jnp.float32),
            pltpu.VMEM((16, 8, LANES), jnp.float32),
            pltpu.VMEM((NF, 8, LANES), jnp.float32),
            whole,
            part_sems,
        ],
        outspecs=HBM,
        cost=3.0,
    )(courant, odd, fe, f, mom, near, zin, joined)
    return untiles(out.reshape(NF * ND, 8, LANES))


def solution(mesh):
    in_specs = (
        P(None, "strip", "pt"),
        P(),
        P("strip", "pt"),
        P("strip", "pt"),
        P("strip", "pt"),
        P("strip", "pt"),
    )
    return jax.shard_map(
        on_device, mesh=mesh, in_specs=in_specs, out_specs=P(None, "strip", "pt"), check_vma=False
    )
```

```python
import jax
import jax.numpy as jnp
import numpy as np
from jax import lax
from jax.experimental import pallas as pl
from jax.experimental.pallas import tpu as pltpu
from jax.sharding import PartitionSpec as P

NF = 25
ND = 24
NG = 3
ROWS = 4
COLS = 256
LANES = 128
PART = 5 * ND * 8
PAD = 1
PAIRED = 2
PER = 5

RATIO = np.float32(1.1) ** np.arange(NF, dtype=np.float32)
THETA = (np.float32(2.0 * np.pi) * np.arange(ND, dtype=np.float32) / np.float32(ND)).astype(np.float32)
COS = np.cos(THETA).astype(np.float32)
SIN = np.sin(THETA).astype(np.float32)
EAST = COS > 0
UP = SIN >= 0
WEIGHT = (RATIO / (np.float32(ND) * RATIO.sum(dtype=np.float32))).astype(np.float32)


def iotas():
    return (
        lax.broadcasted_iota(jnp.int32, (8, LANES), 0),
        lax.broadcasted_iota(jnp.int32, (8, LANES), 1),
    )


def by_sublane(values, sub):
    out = jnp.full((8, LANES), float(values[0]), jnp.float32)
    for j in range(1, 8):
        out = jnp.where(sub == j, float(values[j]), out)
    return out


def direction_tables(sub):
    cu = [by_sublane(np.abs(COS[8 * g : 8 * g + 8]), sub) for g in range(NG)]
    cv = [by_sublane(np.abs(SIN[8 * g : 8 * g + 8]), sub) for g in range(NG)]
    return cu, cv


def east_mask(g, sub):
    if g == 0:
        return sub < 6
    if g == 2:
        return sub >= 2
    return None


def roll(x, shift, axis=1):
    size = x.shape[axis]
    if isinstance(shift, int):
        shift = shift % size
        if shift == 0:
            return x
    return pltpu.roll(x, shift, axis)


def upwind_x(e, edge, sub, lane):
    first, last = lane == 0, lane == LANES - 1
    low, mid, high = e
    both = [jnp.where(sub < 2, high[c], low[c]) for c in (0, 1)]
    both_edge = jnp.where(sub < 2, edge[2], edge[0])

    def from_east(v, beside):
        l0, l1 = roll(v[0], -1), roll(v[1], -1)
        return jnp.where(last, l1, l0), jnp.where(last, beside, l1)

    def from_west(v, beside):
        r0, r1 = roll(v[0], 1), roll(v[1], 1)
        return jnp.where(first, beside, r0), jnp.where(first, r0, r1)

    be, me = from_east(both, both_edge), from_east(mid, edge[1])
    lw, hw = from_west(low, edge[0]), from_west(high, edge[2])
    return [
        [jnp.where(sub < 6, lw[c], be[c]) for c in (0, 1)],
        list(me),
        [jnp.where(sub < 2, be[c], hw[c]) for c in (0, 1)],
    ]


def upwind_y(rows, r, g, sub):
    low = rows[r - 1] if r > 0 else None
    high = rows[r + 1] if r < ROWS - 1 else None
    if g == 0:
        return low
    if g == 2:
        return high
    zero = jnp.zeros((8, LANES), jnp.float32)
    return jnp.where(sub < 4, zero if low is None else low, zero if high is None else high)


def comp_rows(i, g, r, c):
    return pl.ds((i * ND + g * 8) * 8 + c * ROWS + r, 8, 8)


def packed_plus(sub, lane):
    group = (lane // 8) % NG
    d = group * 8 + sub
    return (d < 6) | (d >= 18)


def spread(x, lane):
    x = jnp.where(lane < 8, x, 0.0)
    for step in (8, 16, 32, 64):
        x = x + roll(x, step)
    return x


def edges_kernel(spec_hbm, sea_hbm, x_out, spec, sea, sems):
    sub, lane = iotas()

    def fetch(block):
        part = pl.ds(block * PART, PART)
        return pltpu.make_async_copy(spec_hbm.at[part], spec.at[part], sems.at[block])

    sea_copy = pltpu.make_async_copy(sea_hbm, sea, sems.at[NF // PER])
    sea_copy.start()
    for block in range(NF // PER):
        fetch(block).start()
    here = lane // 2
    shifted = ((lane + 2) & (LANES - 1)) // 2
    plus_at = packed_plus(sub, lane)

    sea_copy.wait()
    seaf = sea[...].astype(jnp.float32)
    slot_e = jnp.zeros((8, LANES), jnp.float32)
    slot_w = jnp.zeros((8, LANES), jnp.float32)
    for r in range(ROWS):
        last = jnp.broadcast_to(roll(seaf, 1)[ROWS + r : ROWS + r + 1, 0:1], (8, LANES))
        first = jnp.broadcast_to(seaf[r : r + 1, 0:1], (8, LANES))
        place = lane // 2 == r
        slot_e = jnp.where(place, last, slot_e)
        slot_w = jnp.where(place, first, slot_w)
    x_out[PER] = spread(slot_e, lane)
    x_out[PER + 1] = spread(slot_w, lane)

    for block in range(NF // PER):
        fetch(block).wait()
        zero = jnp.zeros((8, LANES), jnp.float32)
        easts, wests = [zero] * 3, [zero] * 3
        for t in range(PER):
            i = block * PER + t
            for g in range(NG):
                plus = east_mask(g, sub)
                for r in range(ROWS):
                    v = spec[comp_rows(i, g, r, 0), :]
                    if plus is not None:
                        v = jnp.where(plus, spec[comp_rows(i, g, r, 1), :], v)
                    place = 4 * (NG * t + g) + r
                    v = roll(v, 2 * place)
                    wests[g] = jnp.where(here == place, v, wests[g])
                    if plus is not None:
                        easts[g] = jnp.where(shifted == place, v, easts[g])
        x_out[block] = jnp.where(plus_at, roll(easts[0] + easts[2], 2), wests[0] + wests[1] + wests[2])


def rows_kernel(spec, odd_ref, z_out, a_out):
    sub, _ = iotas()
    odd = odd_ref[0] == 1
    half = sub < 4

    def freqs(block, carry):
        for t in range(PER):
            i = block * PER + t
            load = lambda g, r, c: spec[comp_rows(i, g, r, c), :]
            ups = [load(0, 3, 0), load(0, 3, 1), load(0, 2, 0), load(0, 2, 1)]
            ups += [jnp.where(half, load(1, 3, c), roll(load(1, 2, c), 4, 0)) for c in (0, 1)]
            downs = [load(2, 0, 0), load(2, 0, 1), load(2, 1, 0), load(2, 1, 1)]
            downs += [jnp.where(half, roll(load(1, 1, c), 4, 0), load(1, 0, c)) for c in (0, 1)]
            for j in range(6):
                z_out[i * 6 + j] = jnp.where(odd, ups[j], downs[j])
                a_out[i * 6 + j] = jnp.where(odd, downs[j], ups[j])
        return carry

    lax.fori_loop(0, NF // PER, freqs, 0)


def blocks(body, carry):
    for block in range(NF // PER):
        carry = body(block, carry)
    return carry


def copy_rows(src, dst):
    def some(j, carry):
        for t in range(10):
            dst[j * 10 + t] = src[j * 10 + t]
        return carry

    lax.fori_loop(0, NF * 6 // 10, some, 0)


def join_kernel(second, first, sea, swap_ref, rows, out, rows_out):
    sub, lane = iotas()
    plus = packed_plus(sub, lane)
    swap = swap_ref[0] == 1
    for j in range(PER):
        west = jnp.where(swap, second[j], first[j])
        east = jnp.where(swap, first[j], second[j])
        out[j] = jnp.where(plus, west, east)
    west = jnp.where(swap, second[PER], first[PER])
    east = jnp.where(swap, first[PER + 1], second[PER + 1])
    out[PER] = jnp.where(plus, west, east)
    out[PER + 1] = sea[...].astype(jnp.float32)
    copy_rows(rows, rows_out)
    for j in range(PER):
        rows_out[NF * 6 + j] = out[j]
    rows_out[NF * 6 + PER] = out[PER + 1]
    for j in range(PER + 1, PER + 1 + PAD):
        rows_out[NF * 6 + j] = out[PER]


def append_kernel(rows, joined, out):
    copy_rows(rows, out)
    for j in range(PER):
        out[NF * 6 + j] = joined[j]
    out[NF * 6 + PER] = joined[PER + 1]


def row(x, j):
    return jnp.broadcast_to(x[j : j + 1, :], (8, LANES))


def gain_kernel(ratio_ref, wind_speed, wind_dir, ice, e_in, f_out, fe_out, align):
    sub, lane = iotas()
    icef = ice[...].astype(jnp.float32)
    blow = (1.0 - icef) * 0.05 * wind_speed[...]
    cw, sw = jnp.cos(wind_dir[...]), jnp.sin(wind_dir[...])
    for g in range(NG):
        ct = by_sublane(COS[8 * g : 8 * g + 8], sub)
        st = by_sublane(SIN[8 * g : 8 * g + 8], sub)
        for rc in range(8):
            align[g * 8 + rc] = row(blow, rc) * jnp.maximum(ct * row(cw, rc) + st * row(sw, rc), 0.0)

    def freqs(block, carry):
        for t in range(PER):
            i = block * PER + t
            ratio = ratio_ref[i]
            for rc in range(8):
                cold = 0.7 * row(icef, rc)
                for g in range(NG):
                    at = i * 24 + g * 8 + rc
                    value = jnp.exp(ratio * align[g * 8 + rc] - cold)
                    fe_out[at] = value * e_in[at]
                    r = rc % ROWS
                    if g == 1 or (g == 0) == (r < 2):
                        f_out[at] = value
        return carry

    lax.fori_loop(0, NF // PER, freqs, 0)


def inner_kernel(spec, courant, sea, joined, e_out, mom_out, edge2):
    sub, lane = iotas()
    cu, cv = direction_tables(sub)
    seaf = sea[...].astype(jnp.float32)
    slot = lane // 8
    group = slot % NG
    rr = (lane % 8) // 2
    plus = packed_plus(sub, lane)
    up = group * 8 + sub < 12
    cup = jnp.where(group == 0, cu[0], jnp.where(group == 1, cu[1], cu[2]))
    cvp = jnp.where(group == 0, cv[0], jnp.where(group == 1, cv[1], cv[2]))
    sea_edge = joined[PER]
    for j in range(PER):
        co = jnp.zeros((8, LANES), jnp.float32)
        for t in range(PER):
            co = jnp.where(slot // NG == t, courant[j * PER + t], co)
        au, av = co * cup, co * cvp
        m = joined[j]
        mx = jnp.where(plus, roll(m, 1), roll(m, -1))
        my = jnp.where(up, jnp.where(rr >= 1, roll(m, 2), 0.0), jnp.where(rr <= 2, roll(m, -2), 0.0))
        edge2[j] = sea_edge * ((1.0 - au - av) * m + au * mx + av * my)

    def freqs(block, mom):
        mom = list(mom)
        m1 = joined[block]
        m2 = edge2[block]
        waiting = None

        def put(i, e):
            for g in range(NG):
                for r in range(ROWS):
                    for c in (0, 1):
                        e_out[i * 24 + g * 8 + c * ROWS + r] = e[g][r][c]

        for t in range(PER):
            i = block * PER + t
            ci = courant[i]
            ratio, weight = float(RATIO[i]), float(WEIGHT[i])
            au, av = [ci * x for x in cu], [ci * x for x in cv]
            a0 = [1.0 - x - y for x, y in zip(au, av)]
            e = [[[spec[comp_rows(i, g, r, c), :] for c in (0, 1)] for r in range(ROWS)] for g in range(NG)]
            if waiting is not None:
                put(*waiting)
            for m in (m1, m2):
                new = [[[None, None] for _ in range(ROWS)] for _ in range(NG)]
                for r in range(ROWS):
                    edge = [roll(m, -(8 * (NG * t + g) + 2 * r + 1)) for g in range(NG)]
                    xs = upwind_x([e[g][r] for g in range(NG)], edge, sub, lane)
                    for g in range(NG):
                        for c in (0, 1):
                            val = a0[g] * e[g][r][c] + au[g] * xs[g][c]
                            y = upwind_y([e[g][q][c] for q in range(ROWS)], r, g, sub)
                            if y is not None:
                                val = val + av[g] * y
                            new[g][r][c] = val * row(seaf, c * ROWS + r)
                e = new
            for r in range(ROWS):
                for c in (0, 1):
                    rc = c * ROWS + r
                    wt = weight * (e[0][r][c] + e[1][r][c] + e[2][r][c])
                    mom[rc] = mom[rc] + wt
                    mom[8 + rc] = mom[8 + rc] + wt * ratio
            waiting = (i, e)
        put(*waiting)
        return tuple(mom)

    mom = blocks(freqs, (jnp.zeros((8, LANES), jnp.float32),) * 16)
    for j in range(16):
        mom_out[j] = mom[j]


def side(up, courant, f, msg, joined, fixed, moms, store):
    sub, lane = iotas()
    cu, cv = direction_tables(sub)
    mine = sub < 4 if up else sub >= 4
    first, second, at = (0, 1, 3) if up else (3, 2, 0)
    main = 0 if up else 2
    tail = NF * 6
    sea, sea_edge, beside = joined[PER + 1], joined[PER], msg[tail + PER]
    edge = [roll(sea_edge, -(8 * g + 2 * first + 1)) for g in range(NG)]
    s0 = [row(sea, c * ROWS + first) for c in (0, 1)]
    s1 = [row(sea, c * ROWS + second) for c in (0, 1)]
    sm = [row(beside, c * ROWS + at) for c in (0, 1)]
    masks = {}
    for g in (main, 1):
        sw = upwind_one(s0, edge[g], g, sub, lane)
        masks[g] = [(s0[c] * (s0[c] + sm[c]), s0[c] * (sw[c] + sm[c]), s0[c] * sm[c], s1[c] * s0[c]) for c in (0, 1)]
    masks[1] = [tuple(jnp.where(mine, x, 0.0) for x in masks[1][c]) for c in (0, 1)]

    corners = [roll(msg[tail + block], -(2 * at + 1)) for block in range(NF // PER)]

    def freqs(block, carry):
        moms = list(carry)
        corner = corners[block]
        waiting = []

        def put():
            for where, value in waiting.pop(0):
                fixed[where] = value

        for t in range(PER):
            i = block * PER + t
            ci = courant[i]
            ratio, weight = float(RATIO[i]), float(WEIGHT[i])
            m = [msg[i * 6 + j] for j in range(6)]
            fs = [[[f[i * 24 + g * 8 + c * ROWS + r] for c in (0, 1)] for r in (first, second)] for g in (main, 1)]
            if len(waiting) == 2:
                put()
            total = [[None, None], [None, None]]
            results = []
            for slot, g in enumerate((main, 1)):
                h1 = m[0:2] if slot == 0 else m[4:6]
                h2 = m[2:4] if slot == 0 else [roll(v, 4, 0) for v in m[4:6]]
                hw = upwind_one(h1, roll(corner, -8 * (NG * t + g)), g, sub, lane)
                au, av = ci * cu[g], ci * cv[g]
                a0 = 1.0 - au - av
                k1, k2, k3 = a0 * av, au * av, av * av
                for c in (0, 1):
                    t1, t2, t3, t4 = masks[g][c]
                    adds = (k1 * h1[c] * t1 + k2 * hw[c] * t2 + k3 * h2[c] * t3, k3 * h1[c] * t4)
                    for n, add in enumerate(adds):
                        total[n][c] = add if total[n][c] is None else total[n][c] + add
                        results.append((i * 8 + slot * 4 + n * 2 + c, add * fs[slot][n][c]))
            for n in (0, 1):
                for c in (0, 1):
                    wt = weight * total[n][c]
                    j = n * 2 + c
                    moms[j] = moms[j] + wt
                    moms[4 + j] = moms[4 + j] + wt * ratio
            waiting.append(results)
        while waiting:
            put()
        return tuple(moms)

    rcs = [c * ROWS + r for r in (first, second) for c in (0, 1)]
    start = tuple(moms[rc] for rc in rcs) + tuple(moms[8 + rc] for rc in rcs)
    done = blocks(freqs, start)
    for rc in range(8):
        if rc not in rcs:
            store[rc] = moms[rc]
            store[8 + rc] = moms[8 + rc]
    for j, rc in enumerate(rcs):
        store[rc] = done[j]
        store[8 + rc] = done[4 + j]


def upwind_one(e, edge, g, sub, lane):
    first, last = lane == 0, lane == LANES - 1
    l0, l1 = roll(e[0], -1), roll(e[1], -1)
    x0, x1 = jnp.where(last, l1, l0), jnp.where(last, edge, l1)
    plus = east_mask(g, sub)
    if plus is None:
        return x0, x1
    r0, r1 = roll(e[0], 1), roll(e[1], 1)
    w0, w1 = jnp.where(first, edge, r0), jnp.where(first, r0, r1)
    return jnp.where(plus, w0, x0), jnp.where(plus, w1, x1)


def near_kernel(courant, odd_ref, f, mom, a_in, joined, fixed, mom_out):
    for up in (True, False):

        @pl.when(odd_ref[0] == (1 if up else 0))
        def _():
            side(up, courant, f, a_in, joined, fixed, mom, mom_out)


def outer_kernel(courant, odd_ref, pf, f, mom, near, z_in, joined, out_hbm, far, mom2, growth, out, sems):
    sub, _ = iotas()
    odd = odd_ref[0] == 1
    for up in (True, False):

        @pl.when(odd_ref[0] == (0 if up else 1))
        def _():
            side(up, courant, f, z_in, joined, far, mom, mom2)

    m0 = jnp.zeros((8, LANES), jnp.float32)
    m1 = jnp.zeros((8, LANES), jnp.float32)
    for rc in range(8):
        m0 = jnp.where(sub == rc, jnp.sum(mom2[rc], axis=0, keepdims=True), m0)
        m1 = jnp.where(sub == rc, jnp.sum(mom2[8 + rc], axis=0, keepdims=True), m1)
    loss = 0.02 * (m1 / jnp.maximum(m0, 0.05))
    for i in range(NF):
        growth[i] = jnp.exp(-float(RATIO[i]) * loss)

    def send(block):
        part = pl.ds(pl.multiple_of(block * PART, PART), PART)
        return pltpu.make_async_copy(out.at[part], out_hbm.at[part], sems.at[block])

    def grow(block, carry):
        for t in range(PER):
            i = block * PER + t
            a = [near[i * 8 + j] for j in range(8)]
            z = [far[i * 8 + j] for j in range(8)]
            ups = [jnp.where(odd, x, y) for x, y in zip(a, z)]
            downs = [jnp.where(odd, y, x) for x, y in zip(a, z)]
            for rc in range(8):
                c, r = rc // ROWS, rc % ROWS
                factor = jnp.broadcast_to(growth[i, rc : rc + 1, :], (8, LANES))
                for g in range(NG):
                    val = pf[i * 24 + g * 8 + rc]
                    if r < 2 and g < 2:
                        val = val + ups[(0 if g == 0 else 4) + r * 2 + c]
                    if r >= 2 and g > 0:
                        val = val + downs[(0 if g == 2 else 4) + (3 - r) * 2 + c]
                    out[comp_rows(i, g, r, c), :] = val * factor
        send(block).start()
        return carry

    lax.fori_loop(0, NF // PER, grow, 0)
    for block in range(NF // PER):
        send(block).wait()


VM = pl.BlockSpec(memory_space=pltpu.VMEM)
SM = pl.BlockSpec(memory_space=pltpu.SMEM)
HBM = pl.BlockSpec(memory_space=pltpu.HBM)


def REG(n):
    return jax.ShapeDtypeStruct((n, 8, LANES), jnp.float32)


def call(kernel, outs, ins, scratch=(), vmem=24 << 20, outspecs=None, cost=1.0):
    return pl.pallas_call(
        kernel,
        out_shape=outs,
        in_specs=ins,
        out_specs=jax.tree.map(lambda _: VM, outs) if outspecs is None else outspecs,
        scratch_shapes=list(scratch),
        compiler_params=pltpu.CompilerParams(vmem_limit_bytes=vmem),
        cost_estimate=pl.CostEstimate(flops=0, bytes_accessed=int(cost * 3.6e6), transcendentals=0),
    )


def tiles(x):
    lead = x.shape[:-2]
    x = x.reshape(lead + (ROWS, 2, LANES))
    return jnp.swapaxes(x, -3, -2).reshape(lead + (8, LANES))


def untiles(x):
    lead = x.shape[:-2]
    x = jnp.swapaxes(x.reshape(lead + (2, ROWS, LANES)), -3, -2)
    return x.reshape(lead + (ROWS, COLS))


def on_device(spectra, courant, wind_speed, wind_dir, sea_mask, ice_mask):
    ns, nq = lax.axis_size("strip"), lax.axis_size("pt")
    pair_a = [(i, i ^ 1) for i in range(ns)]
    pair_z = [(i, ((i + 1) ^ 1) - 1) for i in range(1, ns - 1)]
    paired = min(PAIRED, ns)
    east_to = lambda s, p: (((p + 1) ^ 1) - 1) % nq if s < paired else (p + 1) % nq
    west_to = lambda s, p: p ^ 1 if s < paired else (p - 1) % nq
    turn = [[(s * nq + p, s * nq + to(s, p)) for s in range(ns) for p in range(nq)] for to in (east_to, west_to)]
    odd = (lax.axis_index("strip") % 2).reshape(1).astype(jnp.int32)
    swap = ((lax.axis_index("strip") < paired) & (lax.axis_index("pt") % 2 == 1)).reshape(1).astype(jnp.int32)
    ratio = jnp.asarray(RATIO)
    spec = tiles(spectra).reshape(NF * ND * 8, LANES)
    wind_speed, wind_dir, sea, ice = (tiles(x) for x in (wind_speed, wind_dir, sea_mask, ice_mask))
    part_sems = pltpu.SemaphoreType.DMA((NF // PER + 1,))
    whole = pltpu.VMEM((NF * ND * 8, LANES), jnp.float32)
    xmsg = call(edges_kernel, REG(PER + 2), [HBM, HBM], [whole, pltpu.VMEM((8, LANES), jnp.int32), part_sems], cost=2.0, vmem=62 << 20)(spec, sea)
    first, second = (lax.ppermute(xmsg, ("strip", "pt"), t) for t in turn)
    zrows, arows = call(rows_kernel, (REG(NF * 6), REG(NF * 6)), [VM, SM], cost=0.7)(spec, odd)
    joined, zmsg = call(join_kernel, (REG(PER + 2), REG(NF * 6 + PER + 1 + PAD)), [VM, VM, VM, SM, VM], cost=0.2)(second, first, sea, swap, zrows)
    zin = lax.ppermute(zmsg, "strip", pair_z)
    e2, mom = call(
        inner_kernel,
        (REG(NF * 24), REG(16)),
        [VM, SM, VM, VM],
        [pltpu.VMEM((PER, 8, LANES), jnp.float32)],
        cost=5.0,
    )(spec, courant, sea, joined)
    amsg = call(append_kernel, REG(NF * 6 + PER + 1), [VM, VM], cost=0.2)(arows, joined)
    ain = lax.ppermute(amsg, "strip", pair_a)
    ratio, _ = lax.optimization_barrier((ratio, amsg))
    f, fe = call(gain_kernel, (REG(NF * 24), REG(NF * 24)), [SM, VM, VM, VM, VM], [pltpu.VMEM((24, 8, LANES), jnp.float32)], cost=1.0)(
        ratio, wind_speed, wind_dir, ice, e2
    )
    near, mom = call(near_kernel, (REG(NF * 8), REG(16)), [SM, SM, VM, VM, VM, VM], cost=0.0)(courant, odd, f, mom, ain, joined)
    out = call(
        outer_kernel,
        jax.ShapeDtypeStruct((NF * ND * 8, LANES), jnp.float32),
        [SM, SM, VM, VM, VM, VM, VM, VM],
        [
            pltpu.VMEM((NF * 8, 8, LANES), jnp.float32),
            pltpu.VMEM((16, 8, LANES), jnp.float32),
            pltpu.VMEM((NF, 8, LANES), jnp.float32),
            whole,
            part_sems,
        ],
        outspecs=HBM,
        cost=3.0,
    )(courant, odd, fe, f, mom, near, zin, joined)
    return untiles(out.reshape(NF * ND, 8, LANES))


def solution(mesh):
    in_specs = (
        P(None, "strip", "pt"),
        P(),
        P("strip", "pt"),
        P("strip", "pt"),
        P("strip", "pt"),
        P("strip", "pt"),
    )
    return jax.shard_map(
        on_device, mesh=mesh, in_specs=in_specs, out_specs=P(None, "strip", "pt"), check_vma=False
    )
```

```python
import jax
import jax.numpy as jnp
import numpy as np
from jax import lax
from jax.experimental import pallas as pl
from jax.experimental.pallas import tpu as pltpu
from jax.sharding import PartitionSpec as P

NF = 25
ND = 24
NG = 3
ROWS = 4
COLS = 256
LANES = 128
PART = 5 * ND * 8
PAD = 1
PAIRED = 2
PER = 5

RATIO = np.float32(1.1) ** np.arange(NF, dtype=np.float32)
THETA = (np.float32(2.0 * np.pi) * np.arange(ND, dtype=np.float32) / np.float32(ND)).astype(np.float32)
COS = np.cos(THETA).astype(np.float32)
SIN = np.sin(THETA).astype(np.float32)
EAST = COS > 0
UP = SIN >= 0
WEIGHT = (RATIO / (np.float32(ND) * RATIO.sum(dtype=np.float32))).astype(np.float32)


def iotas():
    return (
        lax.broadcasted_iota(jnp.int32, (8, LANES), 0),
        lax.broadcasted_iota(jnp.int32, (8, LANES), 1),
    )


def by_sublane(values, sub):
    out = jnp.full((8, LANES), float(values[0]), jnp.float32)
    for j in range(1, 8):
        out = jnp.where(sub == j, float(values[j]), out)
    return out


def direction_tables(sub):
    cu = [by_sublane(np.abs(COS[8 * g : 8 * g + 8]), sub) for g in range(NG)]
    cv = [by_sublane(np.abs(SIN[8 * g : 8 * g + 8]), sub) for g in range(NG)]
    return cu, cv


def east_mask(g, sub):
    if g == 0:
        return sub < 6
    if g == 2:
        return sub >= 2
    return None


def roll(x, shift, axis=1):
    size = x.shape[axis]
    if isinstance(shift, int):
        shift = shift % size
        if shift == 0:
            return x
    return pltpu.roll(x, shift, axis)


def upwind_x(e, edge, sub, lane):
    first, last = lane == 0, lane == LANES - 1
    low, mid, high = e
    both = [jnp.where(sub < 2, high[c], low[c]) for c in (0, 1)]
    both_edge = jnp.where(sub < 2, edge[2], edge[0])

    def from_east(v, beside):
        l0, l1 = roll(v[0], -1), roll(v[1], -1)
        return jnp.where(last, l1, l0), jnp.where(last, beside, l1)

    def from_west(v, beside):
        r0, r1 = roll(v[0], 1), roll(v[1], 1)
        return jnp.where(first, beside, r0), jnp.where(first, r0, r1)

    be, me = from_east(both, both_edge), from_east(mid, edge[1])
    lw, hw = from_west(low, edge[0]), from_west(high, edge[2])
    return [
        [jnp.where(sub < 6, lw[c], be[c]) for c in (0, 1)],
        list(me),
        [jnp.where(sub < 2, be[c], hw[c]) for c in (0, 1)],
    ]


def upwind_y(rows, r, g, sub):
    low = rows[r - 1] if r > 0 else None
    high = rows[r + 1] if r < ROWS - 1 else None
    if g == 0:
        return low
    if g == 2:
        return high
    zero = jnp.zeros((8, LANES), jnp.float32)
    return jnp.where(sub < 4, zero if low is None else low, zero if high is None else high)


def comp_rows(i, g, r, c):
    return pl.ds((i * ND + g * 8) * 8 + c * ROWS + r, 8, 8)


def packed_plus(sub, lane):
    group = (lane // 8) % NG
    d = group * 8 + sub
    return (d < 6) | (d >= 18)


def spread(x, lane):
    x = jnp.where(lane < 8, x, 0.0)
    for step in (8, 16, 32, 64):
        x = x + roll(x, step)
    return x


def edges_kernel(spec, sea, x_out):
    sub, lane = iotas()
    here = lane // 2
    shifted = ((lane + 2) & (LANES - 1)) // 2
    plus_at = packed_plus(sub, lane)

    seaf = sea[...]
    slot_e = jnp.zeros((8, LANES), jnp.float32)
    slot_w = jnp.zeros((8, LANES), jnp.float32)
    for r in range(ROWS):
        last = jnp.broadcast_to(roll(seaf, 1)[ROWS + r : ROWS + r + 1, 0:1], (8, LANES))
        first = jnp.broadcast_to(seaf[r : r + 1, 0:1], (8, LANES))
        place = lane // 2 == r
        slot_e = jnp.where(place, last, slot_e)
        slot_w = jnp.where(place, first, slot_w)
    x_out[PER] = spread(slot_e, lane)
    x_out[PER + 1] = spread(slot_w, lane)

    for block in range(NF // PER):
        zero = jnp.zeros((8, LANES), jnp.float32)
        easts, wests = [zero] * 3, [zero] * 3
        for t in range(PER):
            i = block * PER + t
            for g in range(NG):
                plus = east_mask(g, sub)
                for r in range(ROWS):
                    v = spec[comp_rows(i, g, r, 0), :]
                    if plus is not None:
                        v = jnp.where(plus, spec[comp_rows(i, g, r, 1), :], v)
                    place = 4 * (NG * t + g) + r
                    v = roll(v, 2 * place)
                    wests[g] = jnp.where(here == place, v, wests[g])
                    if plus is not None:
                        easts[g] = jnp.where(shifted == place, v, easts[g])
        x_out[block] = jnp.where(plus_at, roll(easts[0] + easts[2], 2), wests[0] + wests[1] + wests[2])


def rows_kernel(spec, odd_ref, z_out, a_out):
    sub, _ = iotas()
    odd = odd_ref[0] == 1
    half = sub < 4

    def freqs(block, carry):
        for t in range(PER):
            i = block * PER + t
            load = lambda g, r, c: spec[comp_rows(i, g, r, c), :]
            ups = [load(0, 3, 0), load(0, 3, 1), load(0, 2, 0), load(0, 2, 1)]
            ups += [jnp.where(half, load(1, 3, c), roll(load(1, 2, c), 4, 0)) for c in (0, 1)]
            downs = [load(2, 0, 0), load(2, 0, 1), load(2, 1, 0), load(2, 1, 1)]
            downs += [jnp.where(half, roll(load(1, 1, c), 4, 0), load(1, 0, c)) for c in (0, 1)]
            for j in range(6):
                z_out[i * 6 + j] = jnp.where(odd, ups[j], downs[j])
                a_out[i * 6 + j] = jnp.where(odd, downs[j], ups[j])
        return carry

    lax.fori_loop(0, NF // PER, freqs, 0)


def blocks(body, carry):
    for block in range(NF // PER):
        carry = body(block, carry)
    return carry


def copy_rows(src, dst):
    def some(j, carry):
        for t in range(10):
            dst[j * 10 + t] = src[j * 10 + t]
        return carry

    lax.fori_loop(0, NF * 6 // 10, some, 0)


def join_kernel(second, first, sea, swap_ref, rows, out, rows_out):
    sub, lane = iotas()
    plus = packed_plus(sub, lane)
    swap = swap_ref[0] == 1
    for j in range(PER):
        west = jnp.where(swap, second[j], first[j])
        east = jnp.where(swap, first[j], second[j])
        out[j] = jnp.where(plus, west, east)
    west = jnp.where(swap, second[PER], first[PER])
    east = jnp.where(swap, first[PER + 1], second[PER + 1])
    out[PER] = jnp.where(plus, west, east)
    out[PER + 1] = sea[...]
    copy_rows(rows, rows_out)
    for j in range(PER):
        rows_out[NF * 6 + j] = out[j]
    rows_out[NF * 6 + PER] = out[PER + 1]
    for j in range(PER + 1, PER + 1 + PAD):
        rows_out[NF * 6 + j] = out[PER]


def append_kernel(rows, joined, out):
    copy_rows(rows, out)
    for j in range(PER):
        out[NF * 6 + j] = joined[j]
    out[NF * 6 + PER] = joined[PER + 1]


def row(x, j):
    return jnp.broadcast_to(x[j : j + 1, :], (8, LANES))


def gain_kernel(ratio_ref, wind_speed, wind_dir, ice, e_in, f_out, fe_out, align):
    sub, lane = iotas()
    icef = ice[...].astype(jnp.float32)
    blow = (1.0 - icef) * 0.05 * wind_speed[...]
    cw, sw = jnp.cos(wind_dir[...]), jnp.sin(wind_dir[...])
    for g in range(NG):
        ct = by_sublane(COS[8 * g : 8 * g + 8], sub)
        st = by_sublane(SIN[8 * g : 8 * g + 8], sub)
        for rc in range(8):
            align[g * 8 + rc] = row(blow, rc) * jnp.maximum(ct * row(cw, rc) + st * row(sw, rc), 0.0)

    def freqs(block, carry):
        for t in range(PER):
            i = block * PER + t
            ratio = ratio_ref[i]
            for rc in range(8):
                cold = 0.7 * row(icef, rc)
                for g in range(NG):
                    at = i * 24 + g * 8 + rc
                    value = jnp.exp(ratio * align[g * 8 + rc] - cold)
                    fe_out[at] = value * e_in[at]
                    r = rc % ROWS
                    if g == 1 or (g == 0) == (r < 2):
                        f_out[at] = value
        return carry

    lax.fori_loop(0, NF // PER, freqs, 0)


def inner_kernel(spec, courant, sea, joined, e_out, mom_out, edge2):
    sub, lane = iotas()
    cu, cv = direction_tables(sub)
    seaf = sea[...]
    slot = lane // 8
    group = slot % NG
    rr = (lane % 8) // 2
    plus = packed_plus(sub, lane)
    up = group * 8 + sub < 12
    cup = jnp.where(group == 0, cu[0], jnp.where(group == 1, cu[1], cu[2]))
    cvp = jnp.where(group == 0, cv[0], jnp.where(group == 1, cv[1], cv[2]))
    sea_edge = joined[PER]
    for j in range(PER):
        co = jnp.zeros((8, LANES), jnp.float32)
        for t in range(PER):
            co = jnp.where(slot // NG == t, courant[j * PER + t], co)
        au, av = co * cup, co * cvp
        m = joined[j]
        mx = jnp.where(plus, roll(m, 1), roll(m, -1))
        my = jnp.where(up, jnp.where(rr >= 1, roll(m, 2), 0.0), jnp.where(rr <= 2, roll(m, -2), 0.0))
        edge2[j] = sea_edge * ((1.0 - au - av) * m + au * mx + av * my)

    def freqs(block, mom):
        mom = list(mom)
        m1 = joined[block]
        m2 = edge2[block]
        waiting = None

        def put(i, e):
            for g in range(NG):
                for r in range(ROWS):
                    for c in (0, 1):
                        e_out[i * 24 + g * 8 + c * ROWS + r] = e[g][r][c]

        for t in range(PER):
            i = block * PER + t
            ci = courant[i]
            ratio, weight = float(RATIO[i]), float(WEIGHT[i])
            au, av = [ci * x for x in cu], [ci * x for x in cv]
            a0 = [1.0 - x - y for x, y in zip(au, av)]
            e = [[[spec[comp_rows(i, g, r, c), :] for c in (0, 1)] for r in range(ROWS)] for g in range(NG)]
            if waiting is not None:
                put(*waiting)
            for m in (m1, m2):
                new = [[[None, None] for _ in range(ROWS)] for _ in range(NG)]
                for r in range(ROWS):
                    edge = [roll(m, -(8 * (NG * t + g) + 2 * r + 1)) for g in range(NG)]
                    xs = upwind_x([e[g][r] for g in range(NG)], edge, sub, lane)
                    for g in range(NG):
                        for c in (0, 1):
                            val = a0[g] * e[g][r][c] + au[g] * xs[g][c]
                            y = upwind_y([e[g][q][c] for q in range(ROWS)], r, g, sub)
                            if y is not None:
                                val = val + av[g] * y
                            new[g][r][c] = val * row(seaf, c * ROWS + r)
                e = new
            for r in range(ROWS):
                for c in (0, 1):
                    rc = c * ROWS + r
                    wt = weight * (e[0][r][c] + e[1][r][c] + e[2][r][c])
                    mom[rc] = mom[rc] + wt
                    mom[8 + rc] = mom[8 + rc] + wt * ratio
            waiting = (i, e)
        put(*waiting)
        return tuple(mom)

    mom = blocks(freqs, (jnp.zeros((8, LANES), jnp.float32),) * 16)
    for j in range(16):
        mom_out[j] = mom[j]


def side(up, courant, f, msg, joined, fixed, moms, store):
    sub, lane = iotas()
    cu, cv = direction_tables(sub)
    mine = sub < 4 if up else sub >= 4
    first, second, at = (0, 1, 3) if up else (3, 2, 0)
    main = 0 if up else 2
    tail = NF * 6
    sea, sea_edge, beside = joined[PER + 1], joined[PER], msg[tail + PER]
    edge = [roll(sea_edge, -(8 * g + 2 * first + 1)) for g in range(NG)]
    s0 = [row(sea, c * ROWS + first) for c in (0, 1)]
    s1 = [row(sea, c * ROWS + second) for c in (0, 1)]
    sm = [row(beside, c * ROWS + at) for c in (0, 1)]
    masks = {}
    for g in (main, 1):
        sw = upwind_one(s0, edge[g], g, sub, lane)
        masks[g] = [(s0[c] * (s0[c] + sm[c]), s0[c] * (sw[c] + sm[c]), s0[c] * sm[c], s1[c] * s0[c]) for c in (0, 1)]
    masks[1] = [tuple(jnp.where(mine, x, 0.0) for x in masks[1][c]) for c in (0, 1)]

    corners = [roll(msg[tail + block], -(2 * at + 1)) for block in range(NF // PER)]

    def freqs(block, carry):
        moms = list(carry)
        corner = corners[block]
        waiting = []

        def put():
            for where, value in waiting.pop(0):
                fixed[where] = value

        for t in range(PER):
            i = block * PER + t
            ci = courant[i]
            ratio, weight = float(RATIO[i]), float(WEIGHT[i])
            m = [msg[i * 6 + j] for j in range(6)]
            fs = [[[f[i * 24 + g * 8 + c * ROWS + r] for c in (0, 1)] for r in (first, second)] for g in (main, 1)]
            if len(waiting) == 2:
                put()
            total = [[None, None], [None, None]]
            results = []
            for slot, g in enumerate((main, 1)):
                h1 = m[0:2] if slot == 0 else m[4:6]
                h2 = m[2:4] if slot == 0 else [roll(v, 4, 0) for v in m[4:6]]
                hw = upwind_one(h1, roll(corner, -8 * (NG * t + g)), g, sub, lane)
                au, av = ci * cu[g], ci * cv[g]
                a0 = 1.0 - au - av
                k1, k2, k3 = a0 * av, au * av, av * av
                for c in (0, 1):
                    t1, t2, t3, t4 = masks[g][c]
                    adds = (k1 * h1[c] * t1 + k2 * hw[c] * t2 + k3 * h2[c] * t3, k3 * h1[c] * t4)
                    for n, add in enumerate(adds):
                        total[n][c] = add if total[n][c] is None else total[n][c] + add
                        results.append((i * 8 + slot * 4 + n * 2 + c, add * fs[slot][n][c]))
            for n in (0, 1):
                for c in (0, 1):
                    wt = weight * total[n][c]
                    j = n * 2 + c
                    moms[j] = moms[j] + wt
                    moms[4 + j] = moms[4 + j] + wt * ratio
            waiting.append(results)
        while waiting:
            put()
        return tuple(moms)

    rcs = [c * ROWS + r for r in (first, second) for c in (0, 1)]
    start = tuple(moms[rc] for rc in rcs) + tuple(moms[8 + rc] for rc in rcs)
    done = blocks(freqs, start)
    for rc in range(8):
        if rc not in rcs:
            store[rc] = moms[rc]
            store[8 + rc] = moms[8 + rc]
    for j, rc in enumerate(rcs):
        store[rc] = done[j]
        store[8 + rc] = done[4 + j]


def upwind_one(e, edge, g, sub, lane):
    first, last = lane == 0, lane == LANES - 1
    l0, l1 = roll(e[0], -1), roll(e[1], -1)
    x0, x1 = jnp.where(last, l1, l0), jnp.where(last, edge, l1)
    plus = east_mask(g, sub)
    if plus is None:
        return x0, x1
    r0, r1 = roll(e[0], 1), roll(e[1], 1)
    w0, w1 = jnp.where(first, edge, r0), jnp.where(first, r0, r1)
    return jnp.where(plus, w0, x0), jnp.where(plus, w1, x1)


def near_kernel(courant, odd_ref, f, mom, a_in, joined, fixed, mom_out):
    for up in (True, False):

        @pl.when(odd_ref[0] == (1 if up else 0))
        def _():
            side(up, courant, f, a_in, joined, fixed, mom, mom_out)


def outer_kernel(courant, odd_ref, pf, f, mom, near, z_in, joined, out_hbm, far, mom2, growth, out, sems):
    sub, _ = iotas()
    odd = odd_ref[0] == 1
    for up in (True, False):

        @pl.when(odd_ref[0] == (0 if up else 1))
        def _():
            side(up, courant, f, z_in, joined, far, mom, mom2)

    m0 = jnp.zeros((8, LANES), jnp.float32)
    m1 = jnp.zeros((8, LANES), jnp.float32)
    for rc in range(8):
        m0 = jnp.where(sub == rc, jnp.sum(mom2[rc], axis=0, keepdims=True), m0)
        m1 = jnp.where(sub == rc, jnp.sum(mom2[8 + rc], axis=0, keepdims=True), m1)
    loss = 0.02 * (m1 / jnp.maximum(m0, 0.05))
    for i in range(NF):
        growth[i] = jnp.exp(-float(RATIO[i]) * loss)

    def send(block):
        part = pl.ds(pl.multiple_of(block * PART, PART), PART)
        return pltpu.make_async_copy(out.at[part], out_hbm.at[part], sems.at[block])

    def grow(block, carry):
        for t in range(PER):
            i = block * PER + t
            a = [near[i * 8 + j] for j in range(8)]
            z = [far[i * 8 + j] for j in range(8)]
            ups = [jnp.where(odd, x, y) for x, y in zip(a, z)]
            downs = [jnp.where(odd, y, x) for x, y in zip(a, z)]
            for rc in range(8):
                c, r = rc // ROWS, rc % ROWS
                factor = jnp.broadcast_to(growth[i, rc : rc + 1, :], (8, LANES))
                for g in range(NG):
                    val = pf[i * 24 + g * 8 + rc]
                    if r < 2 and g < 2:
                        val = val + ups[(0 if g == 0 else 4) + r * 2 + c]
                    if r >= 2 and g > 0:
                        val = val + downs[(0 if g == 2 else 4) + (3 - r) * 2 + c]
                    out[comp_rows(i, g, r, c), :] = val * factor
        send(block).start()
        return carry

    lax.fori_loop(0, NF // PER, grow, 0)
    for block in range(NF // PER):
        send(block).wait()


VM = pl.BlockSpec(memory_space=pltpu.VMEM)
SM = pl.BlockSpec(memory_space=pltpu.SMEM)
HBM = pl.BlockSpec(memory_space=pltpu.HBM)


def REG(n):
    return jax.ShapeDtypeStruct((n, 8, LANES), jnp.float32)


def call(kernel, outs, ins, scratch=(), vmem=24 << 20, outspecs=None, cost=1.0):
    return pl.pallas_call(
        kernel,
        out_shape=outs,
        in_specs=ins,
        out_specs=jax.tree.map(lambda _: VM, outs) if outspecs is None else outspecs,
        scratch_shapes=list(scratch),
        compiler_params=pltpu.CompilerParams(vmem_limit_bytes=vmem),
        cost_estimate=pl.CostEstimate(flops=0, bytes_accessed=int(cost * 3.6e6), transcendentals=0),
    )


def tiles(x):
    lead = x.shape[:-2]
    x = x.reshape(lead + (ROWS, 2, LANES))
    return jnp.swapaxes(x, -3, -2).reshape(lead + (8, LANES))


def untiles(x):
    lead = x.shape[:-2]
    x = jnp.swapaxes(x.reshape(lead + (2, ROWS, LANES)), -3, -2)
    return x.reshape(lead + (ROWS, COLS))


def on_device(spectra, courant, wind_speed, wind_dir, sea_mask, ice_mask):
    ns, nq = lax.axis_size("strip"), lax.axis_size("pt")
    pair_a = [(i, i ^ 1) for i in range(ns)]
    pair_z = [(i, ((i + 1) ^ 1) - 1) for i in range(1, ns - 1)]
    paired = min(PAIRED, ns)
    east_to = lambda s, p: (((p + 1) ^ 1) - 1) % nq if s < paired else (p + 1) % nq
    west_to = lambda s, p: p ^ 1 if s < paired else (p - 1) % nq
    turn = [[(s * nq + p, s * nq + to(s, p)) for s in range(ns) for p in range(nq)] for to in (east_to, west_to)]
    odd = (lax.axis_index("strip") % 2).reshape(1).astype(jnp.int32)
    swap = ((lax.axis_index("strip") < paired) & (lax.axis_index("pt") % 2 == 1)).reshape(1).astype(jnp.int32)
    ratio = jnp.asarray(RATIO)
    spec = tiles(spectra).reshape(NF * ND * 8, LANES)
    wind_speed, wind_dir, sea, ice = (tiles(x) for x in (wind_speed, wind_dir, sea_mask.astype(jnp.float32), ice_mask))
    part_sems = pltpu.SemaphoreType.DMA((NF // PER + 1,))
    whole = pltpu.VMEM((NF * ND * 8, LANES), jnp.float32)
    xmsg = call(edges_kernel, REG(PER + 2), [VM, VM], cost=1.0)(spec, sea)
    first, second = (lax.ppermute(xmsg, ("strip", "pt"), t) for t in turn)
    zrows, arows = call(rows_kernel, (REG(NF * 6), REG(NF * 6)), [VM, SM], cost=0.7)(spec, odd)
    joined, zmsg = call(join_kernel, (REG(PER + 2), REG(NF * 6 + PER + 1 + PAD)), [VM, VM, VM, SM, VM], cost=0.2)(second, first, sea, swap, zrows)
    zin = lax.ppermute(zmsg, "strip", pair_z)
    e2, mom = call(
        inner_kernel,
        (REG(NF * 24), REG(16)),
        [VM, SM, VM, VM],
        [pltpu.VMEM((PER, 8, LANES), jnp.float32)],
        cost=5.0,
    )(spec, courant, sea, joined)
    amsg = call(append_kernel, REG(NF * 6 + PER + 1), [VM, VM], cost=0.2)(arows, joined)
    ain = lax.ppermute(amsg, "strip", pair_a)
    ratio, _ = lax.optimization_barrier((ratio, amsg))
    f, fe = call(gain_kernel, (REG(NF * 24), REG(NF * 24)), [SM, VM, VM, VM, VM], [pltpu.VMEM((24, 8, LANES), jnp.float32)], cost=1.0)(
        ratio, wind_speed, wind_dir, ice, e2
    )
    near, mom = call(near_kernel, (REG(NF * 8), REG(16)), [SM, SM, VM, VM, VM, VM], cost=0.0)(courant, odd, f, mom, ain, joined)
    out = call(
        outer_kernel,
        jax.ShapeDtypeStruct((NF * ND * 8, LANES), jnp.float32),
        [SM, SM, VM, VM, VM, VM, VM, VM],
        [
            pltpu.VMEM((NF * 8, 8, LANES), jnp.float32),
            pltpu.VMEM((16, 8, LANES), jnp.float32),
            pltpu.VMEM((NF, 8, LANES), jnp.float32),
            whole,
            part_sems,
        ],
        outspecs=HBM,
        cost=3.0,
    )(courant, odd, fe, f, mom, near, zin, joined)
    return untiles(out.reshape(NF * ND, 8, LANES))


def solution(mesh):
    in_specs = (
        P(None, "strip", "pt"),
        P(),
        P("strip", "pt"),
        P("strip", "pt"),
        P("strip", "pt"),
        P("strip", "pt"),
    )
    return jax.shard_map(
        on_device, mesh=mesh, in_specs=in_specs, out_specs=P(None, "strip", "pt"), check_vma=False
    )
```

```python
import jax
import jax.numpy as jnp
import numpy as np
from jax import lax
from jax.experimental import pallas as pl
from jax.experimental.pallas import tpu as pltpu
from jax.sharding import PartitionSpec as P

NF = 25
ND = 24
NG = 3
ROWS = 4
COLS = 256
LANES = 128
PART = 5 * ND * 8
PAD = 1
PAIRED = 2
PER = 5

RATIO = np.float32(1.1) ** np.arange(NF, dtype=np.float32)
THETA = (np.float32(2.0 * np.pi) * np.arange(ND, dtype=np.float32) / np.float32(ND)).astype(np.float32)
COS = np.cos(THETA).astype(np.float32)
SIN = np.sin(THETA).astype(np.float32)
EAST = COS > 0
UP = SIN >= 0
WEIGHT = (RATIO / (np.float32(ND) * RATIO.sum(dtype=np.float32))).astype(np.float32)


def iotas():
    return (
        lax.broadcasted_iota(jnp.int32, (8, LANES), 0),
        lax.broadcasted_iota(jnp.int32, (8, LANES), 1),
    )


def by_sublane(values, sub):
    out = jnp.full((8, LANES), float(values[0]), jnp.float32)
    for j in range(1, 8):
        out = jnp.where(sub == j, float(values[j]), out)
    return out


def direction_tables(sub):
    cu = [by_sublane(np.abs(COS[8 * g : 8 * g + 8]), sub) for g in range(NG)]
    cv = [by_sublane(np.abs(SIN[8 * g : 8 * g + 8]), sub) for g in range(NG)]
    return cu, cv


def east_mask(g, sub):
    if g == 0:
        return sub < 6
    if g == 2:
        return sub >= 2
    return None


def roll(x, shift, axis=1):
    size = x.shape[axis]
    if isinstance(shift, int):
        shift = shift % size
        if shift == 0:
            return x
    return pltpu.roll(x, shift, axis)


def upwind_x(e, edge, sub, lane):
    first, last = lane == 0, lane == LANES - 1
    low, mid, high = e
    both = [jnp.where(sub < 2, high[c], low[c]) for c in (0, 1)]
    both_edge = jnp.where(sub < 2, edge[2], edge[0])

    def from_east(v, beside):
        l0, l1 = roll(v[0], -1), roll(v[1], -1)
        return jnp.where(last, l1, l0), jnp.where(last, beside, l1)

    def from_west(v, beside):
        r0, r1 = roll(v[0], 1), roll(v[1], 1)
        return jnp.where(first, beside, r0), jnp.where(first, r0, r1)

    be, me = from_east(both, both_edge), from_east(mid, edge[1])
    lw, hw = from_west(low, edge[0]), from_west(high, edge[2])
    return [
        [jnp.where(sub < 6, lw[c], be[c]) for c in (0, 1)],
        list(me),
        [jnp.where(sub < 2, be[c], hw[c]) for c in (0, 1)],
    ]


def upwind_y(rows, r, g, sub):
    low = rows[r - 1] if r > 0 else None
    high = rows[r + 1] if r < ROWS - 1 else None
    if g == 0:
        return low
    if g == 2:
        return high
    zero = jnp.zeros((8, LANES), jnp.float32)
    return jnp.where(sub < 4, zero if low is None else low, zero if high is None else high)


def comp_rows(i, g, r, c):
    return pl.ds((i * ND + g * 8) * 8 + c * ROWS + r, 8, 8)


def packed_plus(sub, lane):
    group = (lane // 8) % NG
    d = group * 8 + sub
    return (d < 6) | (d >= 18)


def spread(x, lane):
    x = jnp.where(lane < 8, x, 0.0)
    for step in (8, 16, 32, 64):
        x = x + roll(x, step)
    return x


def edges_kernel(spec, sea, x_out):
    sub, lane = iotas()
    here = lane // 2
    shifted = ((lane + 2) & (LANES - 1)) // 2
    plus_at = packed_plus(sub, lane)

    seaf = sea[...]
    slot_e = jnp.zeros((8, LANES), jnp.float32)
    slot_w = jnp.zeros((8, LANES), jnp.float32)
    for r in range(ROWS):
        last = jnp.broadcast_to(roll(seaf, 1)[ROWS + r : ROWS + r + 1, 0:1], (8, LANES))
        first = jnp.broadcast_to(seaf[r : r + 1, 0:1], (8, LANES))
        place = lane // 2 == r
        slot_e = jnp.where(place, last, slot_e)
        slot_w = jnp.where(place, first, slot_w)
    x_out[PER] = jnp.where(plus_at, spread(slot_e, lane), spread(slot_w, lane))

    for block in range(NF // PER):
        zero = jnp.zeros((8, LANES), jnp.float32)
        easts, wests = [zero] * 3, [zero] * 3
        for t in range(PER):
            i = block * PER + t
            for g in range(NG):
                plus = east_mask(g, sub)
                for r in range(ROWS):
                    v = spec[comp_rows(i, g, r, 0), :]
                    if plus is not None:
                        v = jnp.where(plus, spec[comp_rows(i, g, r, 1), :], v)
                    place = 4 * (NG * t + g) + r
                    v = roll(v, 2 * place)
                    wests[g] = jnp.where(here == place, v, wests[g])
                    if plus is not None:
                        easts[g] = jnp.where(shifted == place, v, easts[g])
        x_out[block] = jnp.where(plus_at, roll(easts[0] + easts[2], 2), wests[0] + wests[1] + wests[2])


def rows_kernel(spec, odd_ref, z_out, a_out):
    sub, _ = iotas()
    odd = odd_ref[0] == 1
    half = sub < 4

    def freqs(block, carry):
        for t in range(PER):
            i = block * PER + t
            load = lambda g, r, c: spec[comp_rows(i, g, r, c), :]
            ups = [load(0, 3, 0), load(0, 3, 1), load(0, 2, 0), load(0, 2, 1)]
            ups += [jnp.where(half, load(1, 3, c), roll(load(1, 2, c), 4, 0)) for c in (0, 1)]
            downs = [load(2, 0, 0), load(2, 0, 1), load(2, 1, 0), load(2, 1, 1)]
            downs += [jnp.where(half, roll(load(1, 1, c), 4, 0), load(1, 0, c)) for c in (0, 1)]
            for j in range(6):
                z_out[i * 6 + j] = jnp.where(odd, ups[j], downs[j])
                a_out[i * 6 + j] = jnp.where(odd, downs[j], ups[j])
        return carry

    lax.fori_loop(0, NF // PER, freqs, 0)


def blocks(body, carry):
    for block in range(NF // PER):
        carry = body(block, carry)
    return carry


def copy_rows(src, dst):
    def some(j, carry):
        for t in range(10):
            dst[j * 10 + t] = src[j * 10 + t]
        return carry

    lax.fori_loop(0, NF * 6 // 10, some, 0)


def join_kernel(second, first, sea, swap_ref, rows, out, rows_out):
    sub, lane = iotas()
    plus = packed_plus(sub, lane)
    swap = swap_ref[0] == 1
    for j in range(PER):
        west = jnp.where(swap, second[j], first[j])
        east = jnp.where(swap, first[j], second[j])
        out[j] = jnp.where(plus, west, east)
    west = jnp.where(swap, second[PER], first[PER])
    east = jnp.where(swap, first[PER], second[PER])
    out[PER] = jnp.where(plus, west, east)
    out[PER + 1] = sea[...]
    copy_rows(rows, rows_out)
    for j in range(PER):
        rows_out[NF * 6 + j] = out[j]
    rows_out[NF * 6 + PER] = out[PER + 1]
    for j in range(PER + 1, PER + 1 + PAD):
        rows_out[NF * 6 + j] = out[PER]


def append_kernel(rows, joined, out):
    copy_rows(rows, out)
    for j in range(PER):
        out[NF * 6 + j] = joined[j]
    out[NF * 6 + PER] = joined[PER + 1]


def row(x, j):
    return jnp.broadcast_to(x[j : j + 1, :], (8, LANES))


def gain_kernel(ratio_ref, wind_speed, wind_dir, ice, e_in, f_out, fe_out, align):
    sub, lane = iotas()
    icef = ice[...].astype(jnp.float32)
    blow = (1.0 - icef) * 0.05 * wind_speed[...]
    cw, sw = jnp.cos(wind_dir[...]), jnp.sin(wind_dir[...])
    for g in range(NG):
        ct = by_sublane(COS[8 * g : 8 * g + 8], sub)
        st = by_sublane(SIN[8 * g : 8 * g + 8], sub)
        for rc in range(8):
            align[g * 8 + rc] = row(blow, rc) * jnp.maximum(ct * row(cw, rc) + st * row(sw, rc), 0.0)

    def freqs(block, carry):
        for t in range(PER):
            i = block * PER + t
            ratio = ratio_ref[i]
            for rc in range(8):
                cold = 0.7 * row(icef, rc)
                for g in range(NG):
                    at = i * 24 + g * 8 + rc
                    value = jnp.exp(ratio * align[g * 8 + rc] - cold)
                    fe_out[at] = value * e_in[at]
                    r = rc % ROWS
                    if g == 1 or (g == 0) == (r < 2):
                        f_out[at] = value
        return carry

    lax.fori_loop(0, NF // PER, freqs, 0)


def inner_kernel(spec, courant, sea, joined, e_out, mom_out, edge2):
    sub, lane = iotas()
    cu, cv = direction_tables(sub)
    seaf = sea[...]
    slot = lane // 8
    group = slot % NG
    rr = (lane % 8) // 2
    plus = packed_plus(sub, lane)
    up = group * 8 + sub < 12
    cup = jnp.where(group == 0, cu[0], jnp.where(group == 1, cu[1], cu[2]))
    cvp = jnp.where(group == 0, cv[0], jnp.where(group == 1, cv[1], cv[2]))
    sea_edge = joined[PER]
    for j in range(PER):
        co = jnp.zeros((8, LANES), jnp.float32)
        for t in range(PER):
            co = jnp.where(slot // NG == t, courant[j * PER + t], co)
        au, av = co * cup, co * cvp
        m = joined[j]
        mx = jnp.where(plus, roll(m, 1), roll(m, -1))
        my = jnp.where(up, jnp.where(rr >= 1, roll(m, 2), 0.0), jnp.where(rr <= 2, roll(m, -2), 0.0))
        edge2[j] = sea_edge * ((1.0 - au - av) * m + au * mx + av * my)

    def freqs(block, mom):
        mom = list(mom)
        m1 = joined[block]
        m2 = edge2[block]
        waiting = None

        def put(i, e):
            for g in range(NG):
                for r in range(ROWS):
                    for c in (0, 1):
                        e_out[i * 24 + g * 8 + c * ROWS + r] = e[g][r][c]

        for t in range(PER):
            i = block * PER + t
            ci = courant[i]
            ratio, weight = float(RATIO[i]), float(WEIGHT[i])
            au, av = [ci * x for x in cu], [ci * x for x in cv]
            a0 = [1.0 - x - y for x, y in zip(au, av)]
            e = [[[spec[comp_rows(i, g, r, c), :] for c in (0, 1)] for r in range(ROWS)] for g in range(NG)]
            if waiting is not None:
                put(*waiting)
            for m in (m1, m2):
                new = [[[None, None] for _ in range(ROWS)] for _ in range(NG)]
                for r in range(ROWS):
                    edge = [roll(m, -(8 * (NG * t + g) + 2 * r + 1)) for g in range(NG)]
                    xs = upwind_x([e[g][r] for g in range(NG)], edge, sub, lane)
                    for g in range(NG):
                        for c in (0, 1):
                            val = a0[g] * e[g][r][c] + au[g] * xs[g][c]
                            y = upwind_y([e[g][q][c] for q in range(ROWS)], r, g, sub)
                            if y is not None:
                                val = val + av[g] * y
                            new[g][r][c] = val * row(seaf, c * ROWS + r)
                e = new
            for r in range(ROWS):
                for c in (0, 1):
                    rc = c * ROWS + r
                    wt = weight * (e[0][r][c] + e[1][r][c] + e[2][r][c])
                    mom[rc] = mom[rc] + wt
                    mom[8 + rc] = mom[8 + rc] + wt * ratio
            waiting = (i, e)
        put(*waiting)
        return tuple(mom)

    mom = blocks(freqs, (jnp.zeros((8, LANES), jnp.float32),) * 16)
    for j in range(16):
        mom_out[j] = mom[j]


def side(up, courant, f, msg, joined, fixed, moms, store):
    sub, lane = iotas()
    cu, cv = direction_tables(sub)
    mine = sub < 4 if up else sub >= 4
    first, second, at = (0, 1, 3) if up else (3, 2, 0)
    main = 0 if up else 2
    tail = NF * 6
    sea, sea_edge, beside = joined[PER + 1], joined[PER], msg[tail + PER]
    edge = [roll(sea_edge, -(8 * g + 2 * first + 1)) for g in range(NG)]
    s0 = [row(sea, c * ROWS + first) for c in (0, 1)]
    s1 = [row(sea, c * ROWS + second) for c in (0, 1)]
    sm = [row(beside, c * ROWS + at) for c in (0, 1)]
    masks = {}
    for g in (main, 1):
        sw = upwind_one(s0, edge[g], g, sub, lane)
        masks[g] = [(s0[c] * (s0[c] + sm[c]), s0[c] * (sw[c] + sm[c]), s0[c] * sm[c], s1[c] * s0[c]) for c in (0, 1)]
    masks[1] = [tuple(jnp.where(mine, x, 0.0) for x in masks[1][c]) for c in (0, 1)]

    corners = [roll(msg[tail + block], -(2 * at + 1)) for block in range(NF // PER)]

    def freqs(block, carry):
        moms = list(carry)
        corner = corners[block]
        waiting = []

        def put():
            for where, value in waiting.pop(0):
                fixed[where] = value

        for t in range(PER):
            i = block * PER + t
            ci = courant[i]
            ratio, weight = float(RATIO[i]), float(WEIGHT[i])
            m = [msg[i * 6 + j] for j in range(6)]
            fs = [[[f[i * 24 + g * 8 + c * ROWS + r] for c in (0, 1)] for r in (first, second)] for g in (main, 1)]
            if len(waiting) == 2:
                put()
            total = [[None, None], [None, None]]
            results = []
            for slot, g in enumerate((main, 1)):
                h1 = m[0:2] if slot == 0 else m[4:6]
                h2 = m[2:4] if slot == 0 else [roll(v, 4, 0) for v in m[4:6]]
                hw = upwind_one(h1, roll(corner, -8 * (NG * t + g)), g, sub, lane)
                au, av = ci * cu[g], ci * cv[g]
                a0 = 1.0 - au - av
                k1, k2, k3 = a0 * av, au * av, av * av
                for c in (0, 1):
                    t1, t2, t3, t4 = masks[g][c]
                    adds = (k1 * h1[c] * t1 + k2 * hw[c] * t2 + k3 * h2[c] * t3, k3 * h1[c] * t4)
                    for n, add in enumerate(adds):
                        total[n][c] = add if total[n][c] is None else total[n][c] + add
                        results.append((i * 8 + slot * 4 + n * 2 + c, add * fs[slot][n][c]))
            for n in (0, 1):
                for c in (0, 1):
                    wt = weight * total[n][c]
                    j = n * 2 + c
                    moms[j] = moms[j] + wt
                    moms[4 + j] = moms[4 + j] + wt * ratio
            waiting.append(results)
        while waiting:
            put()
        return tuple(moms)

    rcs = [c * ROWS + r for r in (first, second) for c in (0, 1)]
    start = tuple(moms[rc] for rc in rcs) + tuple(moms[8 + rc] for rc in rcs)
    done = blocks(freqs, start)
    for rc in range(8):
        if rc not in rcs:
            store[rc] = moms[rc]
            store[8 + rc] = moms[8 + rc]
    for j, rc in enumerate(rcs):
        store[rc] = done[j]
        store[8 + rc] = done[4 + j]


def upwind_one(e, edge, g, sub, lane):
    first, last = lane == 0, lane == LANES - 1
    l0, l1 = roll(e[0], -1), roll(e[1], -1)
    x0, x1 = jnp.where(last, l1, l0), jnp.where(last, edge, l1)
    plus = east_mask(g, sub)
    if plus is None:
        return x0, x1
    r0, r1 = roll(e[0], 1), roll(e[1], 1)
    w0, w1 = jnp.where(first, edge, r0), jnp.where(first, r0, r1)
    return jnp.where(plus, w0, x0), jnp.where(plus, w1, x1)


def near_kernel(courant, odd_ref, f, mom, a_in, joined, fixed, mom_out):
    for up in (True, False):

        @pl.when(odd_ref[0] == (1 if up else 0))
        def _():
            side(up, courant, f, a_in, joined, fixed, mom, mom_out)


def outer_kernel(courant, odd_ref, pf, f, mom, near, z_in, joined, out_hbm, far, mom2, growth, out, sems):
    sub, _ = iotas()
    odd = odd_ref[0] == 1
    for up in (True, False):

        @pl.when(odd_ref[0] == (0 if up else 1))
        def _():
            side(up, courant, f, z_in, joined, far, mom, mom2)

    m0 = jnp.zeros((8, LANES), jnp.float32)
    m1 = jnp.zeros((8, LANES), jnp.float32)
    for rc in range(8):
        m0 = jnp.where(sub == rc, jnp.sum(mom2[rc], axis=0, keepdims=True), m0)
        m1 = jnp.where(sub == rc, jnp.sum(mom2[8 + rc], axis=0, keepdims=True), m1)
    loss = 0.02 * (m1 / jnp.maximum(m0, 0.05))
    for i in range(NF):
        growth[i] = jnp.exp(-float(RATIO[i]) * loss)

    def send(block):
        part = pl.ds(pl.multiple_of(block * PART, PART), PART)
        return pltpu.make_async_copy(out.at[part], out_hbm.at[part], sems.at[block])

    def grow(block, carry):
        for t in range(PER):
            i = block * PER + t
            a = [near[i * 8 + j] for j in range(8)]
            z = [far[i * 8 + j] for j in range(8)]
            ups = [jnp.where(odd, x, y) for x, y in zip(a, z)]
            downs = [jnp.where(odd, y, x) for x, y in zip(a, z)]
            for rc in range(8):
                c, r = rc // ROWS, rc % ROWS
                factor = jnp.broadcast_to(growth[i, rc : rc + 1, :], (8, LANES))
                for g in range(NG):
                    val = pf[i * 24 + g * 8 + rc]
                    if r < 2 and g < 2:
                        val = val + ups[(0 if g == 0 else 4) + r * 2 + c]
                    if r >= 2 and g > 0:
                        val = val + downs[(0 if g == 2 else 4) + (3 - r) * 2 + c]
                    out[comp_rows(i, g, r, c), :] = val * factor
        send(block).start()
        return carry

    lax.fori_loop(0, NF // PER, grow, 0)
    for block in range(NF // PER):
        send(block).wait()


VM = pl.BlockSpec(memory_space=pltpu.VMEM)
SM = pl.BlockSpec(memory_space=pltpu.SMEM)
HBM = pl.BlockSpec(memory_space=pltpu.HBM)


def REG(n):
    return jax.ShapeDtypeStruct((n, 8, LANES), jnp.float32)


def call(kernel, outs, ins, scratch=(), vmem=24 << 20, outspecs=None, cost=1.0):
    return pl.pallas_call(
        kernel,
        out_shape=outs,
        in_specs=ins,
        out_specs=jax.tree.map(lambda _: VM, outs) if outspecs is None else outspecs,
        scratch_shapes=list(scratch),
        compiler_params=pltpu.CompilerParams(vmem_limit_bytes=vmem),
        cost_estimate=pl.CostEstimate(flops=0, bytes_accessed=int(cost * 3.6e6), transcendentals=0),
    )


def tiles(x):
    lead = x.shape[:-2]
    x = x.reshape(lead + (ROWS, 2, LANES))
    return jnp.swapaxes(x, -3, -2).reshape(lead + (8, LANES))


def untiles(x):
    lead = x.shape[:-2]
    x = jnp.swapaxes(x.reshape(lead + (2, ROWS, LANES)), -3, -2)
    return x.reshape(lead + (ROWS, COLS))


def on_device(spectra, courant, wind_speed, wind_dir, sea_mask, ice_mask):
    ns, nq = lax.axis_size("strip"), lax.axis_size("pt")
    pair_a = [(i, i ^ 1) for i in range(ns)]
    pair_z = [(i, ((i + 1) ^ 1) - 1) for i in range(1, ns - 1)]
    paired = min(PAIRED, ns)
    east_to = lambda s, p: (((p + 1) ^ 1) - 1) % nq if s < paired else (p + 1) % nq
    west_to = lambda s, p: p ^ 1 if s < paired else (p - 1) % nq
    turn = [[(s * nq + p, s * nq + to(s, p)) for s in range(ns) for p in range(nq)] for to in (east_to, west_to)]
    odd = (lax.axis_index("strip") % 2).reshape(1).astype(jnp.int32)
    swap = ((lax.axis_index("strip") < paired) & (lax.axis_index("pt") % 2 == 1)).reshape(1).astype(jnp.int32)
    ratio = jnp.asarray(RATIO)
    spec = tiles(spectra).reshape(NF * ND * 8, LANES)
    wind_speed, wind_dir, sea, ice = (tiles(x) for x in (wind_speed, wind_dir, sea_mask.astype(jnp.float32), ice_mask))
    part_sems = pltpu.SemaphoreType.DMA((NF // PER + 1,))
    whole = pltpu.VMEM((NF * ND * 8, LANES), jnp.float32)
    xmsg = call(edges_kernel, REG(PER + 1), [VM, VM], cost=1.0)(spec, sea)
    first, second = (lax.ppermute(xmsg, ("strip", "pt"), t) for t in turn)
    zrows, arows = call(rows_kernel, (REG(NF * 6), REG(NF * 6)), [VM, SM], cost=0.7)(spec, odd)
    joined, zmsg = call(join_kernel, (REG(PER + 2), REG(NF * 6 + PER + 1 + PAD)), [VM, VM, VM, SM, VM], cost=0.2)(second, first, sea, swap, zrows)
    zin = lax.ppermute(zmsg, "strip", pair_z)
    e2, mom = call(
        inner_kernel,
        (REG(NF * 24), REG(16)),
        [VM, SM, VM, VM],
        [pltpu.VMEM((PER, 8, LANES), jnp.float32)],
        cost=5.0,
    )(spec, courant, sea, joined)
    amsg = call(append_kernel, REG(NF * 6 + PER + 1), [VM, VM], cost=0.2)(arows, joined)
    ain = lax.ppermute(amsg, "strip", pair_a)
    ratio, _ = lax.optimization_barrier((ratio, amsg))
    f, fe = call(gain_kernel, (REG(NF * 24), REG(NF * 24)), [SM, VM, VM, VM, VM], [pltpu.VMEM((24, 8, LANES), jnp.float32)], cost=1.0)(
        ratio, wind_speed, wind_dir, ice, e2
    )
    near, mom = call(near_kernel, (REG(NF * 8), REG(16)), [SM, SM, VM, VM, VM, VM], cost=0.0)(courant, odd, f, mom, ain, joined)
    out = call(
        outer_kernel,
        jax.ShapeDtypeStruct((NF * ND * 8, LANES), jnp.float32),
        [SM, SM, VM, VM, VM, VM, VM, VM],
        [
            pltpu.VMEM((NF * 8, 8, LANES), jnp.float32),
            pltpu.VMEM((16, 8, LANES), jnp.float32),
            pltpu.VMEM((NF, 8, LANES), jnp.float32),
            whole,
            part_sems,
        ],
        outspecs=HBM,
        cost=3.0,
    )(courant, odd, fe, f, mom, near, zin, joined)
    return untiles(out.reshape(NF * ND, 8, LANES))


def solution(mesh):
    in_specs = (
        P(None, "strip", "pt"),
        P(),
        P("strip", "pt"),
        P("strip", "pt"),
        P("strip", "pt"),
        P("strip", "pt"),
    )
    return jax.shard_map(
        on_device, mesh=mesh, in_specs=in_specs, out_specs=P(None, "strip", "pt"), check_vma=False
    )
```
